32 devices in a mesh: slab: 2 (over y), space: 16 (over z, x, core).
Axes of the slice: x: 2, y: 2, z: 4, core: 2. Of those that a mesh axis runs over, the one named last changes fastest.
Arguments:
- snapshots: bfloat16 [2048, 16384], P('space', 'slab'), parts along dimension 1, may hold values from -40 to 40
- weights: float32 [16384], P(('slab', 'space')), parts along dimension 0, may hold values from 0.2 to 2
Outputs:
- modes: bfloat16 [2, 129, 15, 16384], P(None, None, None, ('slab', 'space')), parts along dimension 3
The draws below stay inside these ranges and needn't reach their ends.
There are 2 independent parts, one for each index of `slab`. The reference program is written for one: setup_inputs(seed, part) draws one part's arguments, and reference() takes and returns one part's arrays. A program takes and returns all parts, laid end to end along the dimension named above; each array names one. Nothing has to cross between parts.
All inputs are finite; a program needn't handle non-finite values.
Results may differ from the reference program's by a relative error of at most 0.0063.
Values may be sent and summed in bfloat16 or wider, within the bound.
A program may use at most 64 MiB of HBM per device.

```python
import math
import jax
import jax.numpy as jnp
from jax import lax

SEGMENT_SAMPLES = 256
NB = 15
FREQS = 129
TEMPORAL_SAMPLES = 2048
CELL_DEV = 512
CELLS = 8192


def draw_snapshots(key, part):
    key = jax.random.fold_in(key, 11)
    subkeys = jax.random.split(key, 10)
    sample_moments = jnp.arange(TEMPORAL_SAMPLES, dtype=jnp.float32)
    cell_ids = jnp.arange(CELLS, dtype=jnp.int32)
    rising = 3.0 ** (cell_ids.astype(jnp.float32) / CELLS)
    spread = jnp.exp(jax.random.uniform(subkeys[0], (CELLS,), minval=math.log(0.3), maxval=0.0))
    scaling = rising * spread
    halves_count = TEMPORAL_SAMPLES // (SEGMENT_SAMPLES // 2)
    regions = CELLS // CELL_DEV
    envelope = jnp.exp(0.6 * jnp.clip(jax.random.normal(subkeys[1], (halves_count, regions)), -1.15, 1.15))
    half_ids = jnp.arange(TEMPORAL_SAMPLES, dtype=jnp.int32) // (SEGMENT_SAMPLES // 2)
    region_ids = cell_ids // CELL_DEV
    envelope_full = envelope[half_ids][:, region_ids]
    jitter = jnp.clip(jax.random.normal(subkeys[2], (TEMPORAL_SAMPLES, CELLS)), -4.0, 4.0)
    sampled_record = jnp.zeros((TEMPORAL_SAMPLES, CELLS), jnp.float32)
    for number in range(3):
        angular_speed = jax.random.uniform(subkeys[3 + number], (CELLS,), minval=0.01, maxval=0.45)
        angle_shift = jax.random.uniform(jax.random.fold_in(subkeys[3 + number], 5), (CELLS,), minval=-math.pi, maxval=math.pi)
        oscillation_magnitude = jax.random.uniform(jax.random.fold_in(subkeys[3 + number], 7), (CELLS,), minval=0.3, maxval=1.0)
        sampled_record = sampled_record + oscillation_magnitude * jnp.sin(2.0 * math.pi * angular_speed * sample_moments[:, None] + angle_shift)
    offsets = jax.random.uniform(subkeys[6], (CELLS,), minval=-2.0, maxval=2.0)
    returned_output = offsets + envelope_full * jitter + sampled_record
    return (scaling * returned_output).astype(jnp.bfloat16)


def level_of(key, extent, shards, smallest, largest):
    def one(axis_at, blocks):
        heights = jax.random.uniform(jax.random.fold_in(jax.random.fold_in(key, 6), axis_at), (blocks,), jnp.float32, smallest / len(shards), largest / len(shards))
        return jnp.repeat(jnp.exp(heights), extent[axis_at] // blocks).reshape((-1,) + (1,) * (len(extent) - axis_at - 1))

    loudness = one(*shards[0])
    for cut in shards[1:]:
        loudness = loudness * one(*cut)
    return loudness


def setup_inputs(seed: int = 0, part: int = 0) -> dict:
    splits = jax.random.split(jax.random.key(seed), 3)
    own_keys = jax.random.split(jax.random.fold_in(splits[2], part), 3)
    snapshots = draw_snapshots(jax.random.fold_in(jax.random.fold_in(splits[2], part), 71), part)
    weights = jnp.clip(jnp.exp(math.log(2.0) - 2.3025851 * jax.random.uniform(own_keys[1], (CELLS,), jnp.float32) ** level_of(own_keys[1], (CELLS,), ((0, 16),), -0.2, 0.2)), 0.2, 2.0)
    return {"snapshots": snapshots, "weights": weights}


def make_table():
    sample_moments = jnp.arange(SEGMENT_SAMPLES, dtype=jnp.int32)
    overtone_multiples = jnp.arange(FREQS, dtype=jnp.int32)
    angle_position = overtone_multiples[:, None] * sample_moments[None, :] % SEGMENT_SAMPLES
    phases = 2.0 * math.pi * angle_position.astype(jnp.float32) / SEGMENT_SAMPLES
    taper_weights = 0.5 - 0.5 * jnp.cos(2.0 * math.pi * sample_moments.astype(jnp.float32) / SEGMENT_SAMPLES)
    scaling = 1.0 / math.sqrt(3.0 * SEGMENT_SAMPLES / 8.0)
    table = jnp.stack((taper_weights * jnp.cos(phases) * scaling, -taper_weights * jnp.sin(phases) * scaling))
    table = table.reshape(2 * FREQS, SEGMENT_SAMPLES).astype(jnp.bfloat16)
    row_sums = lax.optimization_barrier(jnp.sum(table.astype(jnp.float32), axis=1))
    return (table, row_sums)

def spectra_of(series, table, row_sums):
    count_snaps, cell_count = series.shape
    average = lax.optimization_barrier(jnp.sum(series.astype(jnp.float32), axis=0)) / count_snaps
    halves = series.reshape(count_snaps // (SEGMENT_SAMPLES // 2), SEGMENT_SAMPLES // 2, cell_count)
    blocks = jnp.concatenate((halves[:-1], halves[1:]), axis=1)
    spectra = jnp.einsum('kt,btc->kbc', table.astype(jnp.float32), blocks.astype(jnp.float32))
    spectra = spectra - row_sums[:, None, None] * average[None, None, :]
    return spectra.reshape(2, FREQS, NB, cell_count)

def gram_parts(weighted):
    wide = weighted.astype(jnp.float32)
    products = jnp.einsum('pfac,qfbc->fpaqb', wide, wide)
    real_part = products[:, 0, :, 0, :] + products[:, 1, :, 1, :]
    imag_part = products[:, 0, :, 1, :] - products[:, 1, :, 0, :]
    return jnp.stack((real_part, imag_part))

def filter_of(gram):
    real_part, imag_part = (gram[0], gram[1])
    level = jnp.trace(real_part, axis1=1, axis2=2) / NB
    identity = jnp.eye(NB, dtype=jnp.float32)
    shifted = real_part + level[:, None, None] * identity
    system = jnp.concatenate((jnp.concatenate((shifted, -imag_part), axis=2), jnp.concatenate((imag_part, shifted), axis=2)), axis=1)
    identity_big = jnp.broadcast_to(jnp.eye(2 * NB, dtype=jnp.float32), system.shape)
    inverse = jnp.linalg.solve(system, identity_big)
    return (identity_big - level[:, None, None] * inverse).astype(jnp.bfloat16)

def reference(snapshots, weights):
    table, row_sums = make_table()
    count_blocks = CELLS // CELL_DEV

    def first_pass(block_index):
        first_cell = block_index * CELL_DEV
        series = lax.dynamic_slice_in_dim(snapshots, first_cell, CELL_DEV, 1)
        local_weights = lax.dynamic_slice_in_dim(weights, first_cell, CELL_DEV, 0)
        spectra = spectra_of(series, table, row_sums)
        weighted = (spectra * jnp.sqrt(local_weights)).astype(jnp.bfloat16)
        return (weighted, gram_parts(weighted))
    weighted_all, grams = lax.map(first_pass, jnp.arange(count_blocks, dtype=jnp.int32))
    filters = filter_of(lax.optimization_barrier(jnp.sum(grams, axis=0))).astype(jnp.float32)
    filters_five = filters.reshape(FREQS, 2, NB, 2, NB)

    def second_pass(pair):
        weighted, local_weights = pair
        mixed = jnp.einsum('fpaqb,pfac->qfbc', filters_five, weighted.astype(jnp.float32))
        return (mixed / jnp.sqrt(local_weights)).astype(jnp.bfloat16)
    outputs = lax.map(second_pass, (weighted_all, weights.reshape(count_blocks, CELL_DEV)))
    return outputs.transpose(1, 2, 3, 0, 4).reshape(2, FREQS, NB, CELLS)
```

```python
import functools
import math

import jax
import jax.numpy as jnp
import numpy as np
import ml_dtypes
from jax import lax
from jax.experimental import pallas as pl
from jax.experimental.pallas import tpu as pltpu
from jax.sharding import PartitionSpec as P

SEG = 256
HALF = SEG // 2
NB = 15
FREQS = 129
NBP = 16
GROUP = 8
GROUPS = -(-FREQS // GROUP)
FP = GROUPS * GROUP
LANES = 128
MESH = pl.DeviceIdType.MESH
VMEM = pl.BlockSpec(memory_space=pltpu.VMEM)


def make_table():
    t = np.arange(SEG)
    k = np.arange(FREQS)
    phases = 2.0 * np.pi * (k[:, None] * t[None, :] % SEG) / SEG
    taper = 0.5 - 0.5 * np.cos(2.0 * np.pi * t / SEG)
    scaling = 1.0 / math.sqrt(3.0 * SEG / 8.0)
    table = np.zeros((2, FP, SEG), np.float32)
    table[0, :FREQS] = taper * np.cos(phases) * scaling
    table[1, :FREQS] = -taper * np.sin(phases) * scaling
    return table.reshape(2 * FP, SEG).astype(ml_dtypes.bfloat16)


def gram_rows(n):
    return -(-(GROUPS * 2 * NBP // 8) // n) * 8


def dft_chunk(tab_ref, x_ref, w_ref, s_ref, lane0, width):
    tab = tab_ref[...]
    row_sums = jnp.sum(tab.astype(jnp.float32), axis=1, keepdims=True)
    cols = pl.ds(lane0, width)
    average = jnp.sum(x_ref[:, cols].astype(jnp.float32), axis=0, keepdims=True) / x_ref.shape[0]
    root = jnp.sqrt(w_ref[:, cols])
    corr = row_sums * (average * root)
    for b in range(NB):
        sp = jnp.dot(tab, x_ref[b * HALF : b * HALF + SEG, cols], preferred_element_type=jnp.float32)
        sp = sp * root - corr
        for p in range(2):
            for i in range(width // LANES):
                s_ref[p, lane0 // LANES + i, pl.ds(b, FP, stride=NBP), :] = sp[
                    p * FP : (p + 1) * FP, i * LANES : (i + 1) * LANES
                ]
    for p in range(2):
        for i in range(width // LANES):
            s_ref[p, lane0 // LANES + i, pl.ds(NB, FP, stride=NBP), :] = jnp.zeros((FP, LANES), jnp.float32)


def gram_group(s_ref, wtd_ref, g_ref, chunks, g):
    rows = pl.ds(pl.multiple_of(g * LANES, LANES), LANES)
    parts = [
        jnp.concatenate([s_ref[p, i, rows, :] for i in range(chunks)], axis=1).astype(jnp.bfloat16)
        for p in range(2)
    ]
    for p in range(2):
        wtd_ref[p, pl.ds(pl.multiple_of(g * GROUP, GROUP), GROUP)] = parts[p].reshape(
            GROUP, NBP, chunks * LANES
        )
    x = jnp.concatenate(parts, axis=0)
    prod = lax.dot_general(x, x, (((1,), (1,)), ((), ())), preferred_element_type=jnp.float32)
    re = prod[:LANES, :LANES] + prod[LANES:, LANES:]
    im = prod[:LANES, LANES:] - prod[LANES:, :LANES]
    freq = lax.broadcasted_iota(jnp.int32, (NBP, LANES), 1) // NBP
    for part, full in enumerate((re, im)):
        folded = jnp.zeros((NBP, LANES), jnp.float32)
        for k in range(GROUP):
            folded = jnp.where(freq == k, full[k * NBP : (k + 1) * NBP], folded)
        g_ref[pl.ds(pl.multiple_of(g * 2 * NBP + part * NBP, NBP), NBP), :] = folded


def spectra_kernel(tab_ref, x_ref, w_ref, wtd_ref, g_ref, s_ref):
    cells = x_ref.shape[1]
    for lane0 in range(0, cells, 256):
        dft_chunk(tab_ref, x_ref, w_ref, s_ref, lane0, 256)
    used = GROUPS * 2 * NBP
    if g_ref.shape[0] > used:
        g_ref[used:, :] = jnp.zeros((g_ref.shape[0] - used, LANES), jnp.float32)

    @pl.loop(0, GROUPS)
    def _(g):
        gram_group(s_ref, wtd_ref, g_ref, cells // LANES, g)


def sum_kernel(n, g_ref, out_ref, got_ref, own_ref, send1, recv1, send2, recv2):
    me = lax.axis_index("space")
    share = g_ref.shape[0] // n
    mine = pl.ds(pl.multiple_of(me * share, 8), share)

    def peer(i):
        return lax.rem(me + i, n)

    barrier = pltpu.get_barrier_semaphore()

    @pl.loop(1, n)
    def _(i):
        pl.semaphore_signal(barrier, inc=1, device_id={"space": peer(i)}, device_id_type=MESH)

    pl.semaphore_wait(barrier, n - 1)

    def scatter(i):
        there = peer(i)
        return pltpu.make_async_remote_copy(
            src_ref=g_ref.at[pl.ds(pl.multiple_of(there * share, 8), share)],
            dst_ref=got_ref.at[i],
            send_sem=send1.at[i],
            recv_sem=recv1.at[i],
            device_id={"space": there},
            device_id_type=MESH,
        )

    def gather(i):
        return pltpu.make_async_remote_copy(
            src_ref=own_ref,
            dst_ref=out_ref.at[mine],
            send_sem=send2.at[i],
            recv_sem=recv2.at[i],
            device_id={"space": peer(i)},
            device_id_type=MESH,
        )

    @pl.loop(1, n)
    def _(i):
        scatter(i).start()

    own_ref[...] = g_ref[mine, :]

    @pl.loop(1, n)
    def _(i):
        scatter(i).wait_recv()
        own_ref[...] += got_ref[i]

    @pl.loop(1, n)
    def _(i):
        gather(i).start()

    out_ref[mine, :] = own_ref[...]

    @pl.loop(1, n)
    def _(i):
        scatter(i).wait_send()
        gather(i).wait()


def group_sum(x, lane):
    for step in (1, 2, 4, 8):
        x = x + jnp.take_along_axis(x, jnp.bitwise_xor(lane, step), axis=1)
    return x


def invert(g_ref, f_ref):
    shape = (GROUPS, NBP, LANES)
    flat = (GROUPS * NBP, LANES)
    packed = g_ref[: GROUPS * 2 * NBP, :].reshape(GROUPS, 2, NBP, LANES)
    re, im = packed[:, 0], packed[:, 1]
    row = lax.broadcasted_iota(jnp.int32, (1, NBP, LANES), 1)
    lane = lax.broadcasted_iota(jnp.int32, (1, NBP, LANES), 2)
    col = lane % NBP
    lane_flat = lax.broadcasted_iota(jnp.int32, flat, 1)
    base = lane_flat - lane_flat % NBP
    diag = row == col
    trace = jnp.sum(jnp.where(diag, re, 0.0), axis=1, keepdims=True)
    level = group_sum(jnp.broadcast_to(trace, shape).reshape(flat), lane_flat).reshape(shape) / NB
    group = lax.broadcasted_iota(jnp.int32, shape, 0)
    real = group * GROUP + lax.broadcasted_iota(jnp.int32, shape, 2) // NBP < FREQS
    level = jnp.where(real, level, 1.0)
    re = re + jnp.where(diag, level, 0.0)
    for j in range(NB):
        index = base + j
        col_re = jnp.take_along_axis(re.reshape(flat), index, axis=1).reshape(shape)
        col_im = jnp.take_along_axis(im.reshape(flat), index, axis=1).reshape(shape)
        inverse = 1.0 / col_re[:, j : j + 1]
        here = (col == j)[:, j : j + 1]
        row_re = jnp.where(here, inverse, re[:, j : j + 1] * inverse)
        row_im = jnp.where(here, 0.0, im[:, j : j + 1] * inverse)
        cross = (row == j) | (col == j)
        col_re = jnp.where(row == j, -1.0, col_re)
        col_im = jnp.where(row == j, 0.0, col_im)
        re = jnp.where(cross, 0.0, re) - (col_re * row_re - col_im * row_im)
        im = jnp.where(cross, 0.0, im) - (col_re * row_im + col_im * row_re)
    f_ref[:, 0] = jnp.where(diag, 1.0, 0.0) - level * re
    f_ref[:, 1] = level * im


def modes_kernel(g_ref, w_ref, wtd_ref, out_ref, f_ref):
    g = pl.program_id(0)

    @pl.when(g == 0)
    def _():
        invert(g_ref, f_ref)

    cells = w_ref.shape[1]
    inverse_root = 1.0 / jnp.sqrt(w_ref[...])
    own = (
        lax.broadcasted_iota(jnp.int32, (LANES, LANES), 0) // NBP
        == lax.broadcasted_iota(jnp.int32, (LANES, LANES), 1) // NBP
    )
    same = jnp.where(own, jnp.concatenate([f_ref[g, 0]] * GROUP, axis=0), 0.0).astype(jnp.bfloat16)
    other = jnp.where(own, jnp.concatenate([f_ref[g, 1]] * GROUP, axis=0), 0.0).astype(jnp.bfloat16)
    filters = jnp.concatenate(
        (jnp.concatenate((same, other), axis=1), jnp.concatenate((-other, same), axis=1)), axis=0
    )
    wtd = wtd_ref[...].reshape(2 * LANES, cells)
    mixed = jnp.dot(filters, wtd, preferred_element_type=jnp.float32) * inverse_root
    mixed = mixed.astype(jnp.bfloat16).reshape(2, GROUP, NBP, cells)
    out_ref[...] = mixed[:, :, :NB]


def per_device(snapshots, weights):
    n = lax.axis_size("space")
    cells = snapshots.shape[1] // n
    table = jnp.asarray(make_table())
    shaped = snapshots.reshape(snapshots.shape[0], n, cells)
    columns = lax.all_to_all(shaped, "space", split_axis=1, concat_axis=0, tiled=True)
    x = columns[:, 0, :]
    w = weights.reshape(1, cells)
    share = gram_rows(n)
    wtd, gram = pl.pallas_call(
        spectra_kernel,
        out_shape=(
            jax.ShapeDtypeStruct((2, FP, NBP, cells), jnp.bfloat16),
            jax.ShapeDtypeStruct((n * share, LANES), jnp.float32),
        ),
        in_specs=[VMEM] * 3,
        out_specs=(VMEM, VMEM),
        scratch_shapes=[pltpu.VMEM((2, cells // LANES, FP * NBP, LANES), jnp.float32)],
        compiler_params=pltpu.CompilerParams(vmem_limit_bytes=40 << 20),
        name="spectra",
    )(table, x, w)
    total = pl.pallas_call(
        functools.partial(sum_kernel, n),
        out_shape=jax.ShapeDtypeStruct((n * share, LANES), jnp.float32),
        in_specs=[VMEM],
        out_specs=VMEM,
        scratch_shapes=[
            pltpu.VMEM((n, share, LANES), jnp.float32),
            pltpu.VMEM((share, LANES), jnp.float32),
        ]
        + [pltpu.SemaphoreType.DMA((n,))] * 4,
        compiler_params=pltpu.CompilerParams(collective_id=0, has_side_effects=True),
        name="gram_sum",
    )(gram)
    return pl.pallas_call(
        modes_kernel,
        grid=(GROUPS,),
        out_shape=jax.ShapeDtypeStruct((2, FREQS, NB, cells), jnp.bfloat16),
        in_specs=[
            VMEM,
            VMEM,
            pl.BlockSpec((2, GROUP, NBP, cells), lambda g: (0, g, 0, 0)),
        ],
        out_specs=pl.BlockSpec((2, GROUP, NB, cells), lambda g: (0, g, 0, 0)),
        scratch_shapes=[pltpu.VMEM((GROUPS, 2, NBP, LANES), jnp.float32)],
        compiler_params=pltpu.CompilerParams(vmem_limit_bytes=32 << 20),
        name="modes",
    )(total, w, wtd)


def solution(mesh):
    return jax.shard_map(
        per_device,
        mesh=mesh,
        in_specs=(P("space", "slab"), P(("slab", "space"))),
        out_specs=P(None, None, None, ("slab", "space")),
        check_vma=False,
    )
```

```python
import functools
import math

import jax
import jax.numpy as jnp
import numpy as np
import ml_dtypes
from jax import lax
from jax.experimental import pallas as pl
from jax.experimental.pallas import tpu as pltpu
from jax.sharding import PartitionSpec as P

SEG = 256
HALF = SEG // 2
NB = 15
FREQS = 129
NBP = 16
GROUP = 8
GROUPS = -(-FREQS // GROUP)
FP = GROUPS * GROUP
LANES = 128
MESH = pl.DeviceIdType.MESH
VMEM = pl.BlockSpec(memory_space=pltpu.VMEM)


def make_table():
    t = np.arange(SEG)
    k = np.arange(FREQS)
    phases = 2.0 * np.pi * (k[:, None] * t[None, :] % SEG) / SEG
    taper = 0.5 - 0.5 * np.cos(2.0 * np.pi * t / SEG)
    scaling = 1.0 / math.sqrt(3.0 * SEG / 8.0)
    table = np.zeros((2, FP, SEG), np.float32)
    table[0, :FREQS] = taper * np.cos(phases) * scaling
    table[1, :FREQS] = -taper * np.sin(phases) * scaling
    return table.reshape(2 * FP, SEG).astype(ml_dtypes.bfloat16)


CHUNK = 256


def dft_chunk(tab_ref, x_ref, w_ref, s_ref, h):
    tab = tab_ref[...]
    row_sums = jnp.sum(tab.astype(jnp.float32), axis=1, keepdims=True)
    average = jnp.sum(x_ref[h].astype(jnp.float32), axis=0, keepdims=True) / x_ref.shape[1]
    root = jnp.sqrt(w_ref[:, pl.ds(pl.multiple_of(h * CHUNK, CHUNK), CHUNK)])
    corr = row_sums * (average * root)
    for b in range(NB):
        sp = jnp.dot(tab, x_ref[h, b * HALF : b * HALF + SEG, :], preferred_element_type=jnp.float32)
        sp = sp * root - corr
        for p in range(2):
            for i in range(CHUNK // LANES):
                s_ref[p, i, pl.ds(b, FP, stride=NBP), :] = sp[
                    p * FP : (p + 1) * FP, i * LANES : (i + 1) * LANES
                ]


def gram_group(s_ref, wtd_ref, g_ref, h, g):
    rows = pl.ds(pl.multiple_of(g * LANES, LANES), LANES)
    cols = pl.ds(pl.multiple_of(h * CHUNK, CHUNK), CHUNK)
    parts = [
        jnp.concatenate([s_ref[p, i, rows, :] for i in range(CHUNK // LANES)], axis=1).astype(jnp.bfloat16)
        for p in range(2)
    ]
    for p in range(2):
        wtd_ref[p, pl.ds(pl.multiple_of(g * GROUP, GROUP), GROUP), :, cols] = parts[p].reshape(
            GROUP, NBP, CHUNK
        )
    x = jnp.concatenate(parts, axis=0)
    prod = lax.dot_general(x, x, (((1,), (1,)), ((), ())), preferred_element_type=jnp.float32)
    re = prod[:LANES, :LANES] + prod[LANES:, LANES:]
    im = prod[:LANES, LANES:] - prod[LANES:, :LANES]
    freq = lax.broadcasted_iota(jnp.int32, (NBP, LANES), 1) // NBP
    for part, full in enumerate((re, im)):
        folded = jnp.zeros((NBP, LANES), jnp.float32)
        for k in range(GROUP):
            folded = jnp.where(freq == k, full[k * NBP : (k + 1) * NBP], folded)
        g_ref[g, part] += folded


def group_sum(x, lane):
    for step in (1, 2, 4, 8):
        x = x + jnp.take_along_axis(x, jnp.bitwise_xor(lane, step), axis=1)
    return x


def invert(re, im, real):
    shape = re.shape
    flat = (shape[0] * NBP, LANES)
    row = lax.broadcasted_iota(jnp.int32, (1, NBP, LANES), 1)
    lane = lax.broadcasted_iota(jnp.int32, (1, NBP, LANES), 2)
    col = lane % NBP
    lane_flat = lax.broadcasted_iota(jnp.int32, flat, 1)
    base = lane_flat - lane_flat % NBP
    diag = row == col
    trace = jnp.sum(jnp.where(diag, re, 0.0), axis=1, keepdims=True)
    level = group_sum(jnp.broadcast_to(trace, shape).reshape(flat), lane_flat).reshape(shape) / NB
    level = jnp.where(real, level, 1.0)
    re = re + jnp.where(diag, level, 0.0)
    for j in range(NB):
        index = base + j
        col_re = jnp.take_along_axis(re.reshape(flat), index, axis=1).reshape(shape)
        col_im = jnp.take_along_axis(im.reshape(flat), index, axis=1).reshape(shape)
        inverse = 1.0 / col_re[:, j : j + 1]
        here = (col == j)[:, j : j + 1]
        row_re = jnp.where(here, inverse, re[:, j : j + 1] * inverse)
        row_im = jnp.where(here, 0.0, im[:, j : j + 1] * inverse)
        cross = (row == j) | (col == j)
        col_re = jnp.where(row == j, -1.0, col_re)
        col_im = jnp.where(row == j, 0.0, col_im)
        re = jnp.where(cross, 0.0, re) - (col_re * row_re - col_im * row_im)
        im = jnp.where(cross, 0.0, im) - (col_re * row_im + col_im * row_re)
    return jnp.where(diag, 1.0, 0.0) - level * re, level * im


def filters_kernel(
    n, snap_ref, tab_ref, w_ref, wtd_ref, f_ref,
    x_ref, s_ref, g_ref, got_ref, tot_ref,
    x_own, x_send, x_recv, g_send, g_recv, f_send, f_recv,
):
    me = lax.axis_index("space")
    rows = snap_ref.shape[0]
    cells = w_ref.shape[1]
    pieces = cells // CHUNK
    slots = -(-GROUPS // n)

    def peer(i):
        return lax.rem(me + i, n)

    def piece(there, h):
        return snap_ref.at[:, pl.ds(pl.multiple_of(there * cells + h * CHUNK, CHUNK), CHUNK)]

    x_mine = pl.ds(pl.multiple_of(me * rows, rows), rows)

    def local(h):
        return pltpu.make_async_copy(piece(me, h), x_ref.at[h, x_mine], x_own.at[h])

    def exchange(i, h):
        there = peer(i)
        return pltpu.make_async_remote_copy(
            src_ref=piece(there, h),
            dst_ref=x_ref.at[h, x_mine],
            send_sem=x_send.at[h, i],
            recv_sem=x_recv.at[h, i],
            device_id={"space": there},
            device_id_type=MESH,
        )

    def scatter(g):
        return pltpu.make_async_remote_copy(
            src_ref=g_ref.at[g],
            dst_ref=got_ref.at[g // n, me],
            send_sem=g_send.at[g],
            recv_sem=g_recv.at[g // n, me],
            device_id={"space": lax.rem(g, n)},
            device_id_type=MESH,
        )

    def scattered(slot, source):
        return pltpu.make_async_remote_copy(
            src_ref=g_ref.at[0],
            dst_ref=got_ref.at[slot, source],
            send_sem=g_send.at[0],
            recv_sem=g_recv.at[slot, source],
            device_id={"space": source},
            device_id_type=MESH,
        )

    def gather(g, i):
        return pltpu.make_async_remote_copy(
            src_ref=f_ref.at[g],
            dst_ref=f_ref.at[g],
            send_sem=f_send.at[g // n, i],
            recv_sem=f_recv.at[g],
            device_id={"space": peer(i)},
            device_id_type=MESH,
        )

    barrier = pltpu.get_barrier_semaphore()

    @pl.loop(1, n)
    def _(i):
        pl.semaphore_signal(barrier, inc=1, device_id={"space": peer(i)}, device_id_type=MESH)

    for h in range(pieces):
        local(h).start()
    pl.semaphore_wait(barrier, n - 1)

    @pl.loop(0, pieces)
    def _(h):
        @pl.loop(1, n)
        def _(i):
            exchange(i, h).start()

    g_ref[...] = jnp.zeros_like(g_ref)
    for p in range(2):
        for i in range(CHUNK // LANES):
            s_ref[p, i, pl.ds(NB, FP, stride=NBP), :] = jnp.zeros((FP, LANES), jnp.float32)

    @pl.loop(0, pieces)
    def _(h):
        @pl.loop(1, n)
        def _(i):
            exchange(i, h).wait_recv()

        local(h).wait()
        dft_chunk(tab_ref, x_ref, w_ref, s_ref, h)

        @pl.loop(0, GROUPS)
        def _(g):
            gram_group(s_ref, wtd_ref, g_ref, h, g)

            @pl.when(jnp.logical_and(h == pieces - 1, lax.rem(g, n) != me))
            def _():
                scatter(g).start()

    for slot in range(slots):
        g = slot * n + me

        @pl.when(g < GROUPS)
        def _():
            tot_ref[slot] = g_ref[g]

            @pl.loop(1, n)
            def _(i):
                source = peer(i)
                scattered(slot, source).wait_recv()
                tot_ref[slot] += got_ref[slot, source]

        @pl.when(g >= GROUPS)
        def _():
            tot_ref[slot] = jnp.zeros((2, NBP, LANES), jnp.float32)

    shape = (slots, NBP, LANES)
    freq = (lax.broadcasted_iota(jnp.int32, shape, 0) * n + me) * GROUP + lax.broadcasted_iota(
        jnp.int32, shape, 2
    ) // NBP
    same, other = invert(tot_ref[:, 0], tot_ref[:, 1], freq < FREQS)
    for slot in range(slots):
        g = slot * n + me

        @pl.when(g < GROUPS)
        def _():
            f_ref[g, 0] = same[slot].astype(jnp.bfloat16)
            f_ref[g, 1] = other[slot].astype(jnp.bfloat16)

            @pl.loop(1, n)
            def _(i):
                gather(g, i).start()

    @pl.loop(0, pieces)
    def _(h):
        @pl.loop(1, n)
        def _(i):
            exchange(i, h).wait_send()

    @pl.loop(0, GROUPS)
    def _(g):
        @pl.when(lax.rem(g, n) != me)
        def _():
            scatter(g).wait_send()
            gather(g, 0).wait_recv()

    for slot in range(slots):
        g = slot * n + me

        @pl.when(g < GROUPS)
        def _():
            @pl.loop(1, n)
            def _(i):
                gather(g, i).wait_send()


def modes_kernel(f_ref, w_ref, wtd_ref, out_ref, mix_ref):
    cells = w_ref.shape[1]
    inverse_root = 1.0 / jnp.sqrt(w_ref[...])
    own = (
        lax.broadcasted_iota(jnp.int32, (LANES, LANES), 0) // NBP
        == lax.broadcasted_iota(jnp.int32, (LANES, LANES), 1) // NBP
    )
    same, other = (
        jnp.where(own, jnp.concatenate([f_ref[0, part].astype(jnp.float32)] * GROUP, axis=0), 0.0)
        for part in range(2)
    )
    mix_ref[0, pl.ds(0, LANES, stride=2), :] = same
    mix_ref[0, pl.ds(1, LANES, stride=2), :] = -other
    mix_ref[1, pl.ds(0, LANES, stride=2), :] = other
    mix_ref[1, pl.ds(1, LANES, stride=2), :] = same
    filters = jnp.concatenate((mix_ref[0], mix_ref[1]), axis=1).astype(jnp.bfloat16)
    wtd = wtd_ref[...].reshape(2 * LANES, cells)
    mixed = jnp.dot(filters, wtd, preferred_element_type=jnp.float32) * inverse_root
    mixed = mixed.astype(jnp.bfloat16).reshape(GROUP, NBP, 2, cells)
    out_ref[...] = mixed[:, :NB]


def per_device(snapshots, weights):
    n = lax.axis_size("space")
    rows = snapshots.shape[0]
    cells = snapshots.shape[1] // n
    pieces = cells // CHUNK
    slots = -(-GROUPS // n)
    table = jnp.asarray(make_table())
    w = weights.reshape(1, cells)
    dma = pltpu.SemaphoreType.DMA
    wtd, filters = pl.pallas_call(
        functools.partial(filters_kernel, n),
        out_shape=(
            jax.ShapeDtypeStruct((2, FP, NBP, cells), jnp.bfloat16),
            jax.ShapeDtypeStruct((GROUPS, 2, NBP, LANES), jnp.bfloat16),
        ),
        in_specs=[pl.BlockSpec(memory_space=pl.ANY), VMEM, VMEM],
        out_specs=(VMEM, VMEM),
        scratch_shapes=[
            pltpu.VMEM((pieces, n * rows, CHUNK), jnp.bfloat16),
            pltpu.VMEM((2, CHUNK // LANES, FP * NBP, LANES), jnp.float32),
            pltpu.VMEM((GROUPS, 2, NBP, LANES), jnp.float32),
            pltpu.VMEM((slots, n, 2, NBP, LANES), jnp.float32),
            pltpu.VMEM((slots, 2, NBP, LANES), jnp.float32),
            dma((pieces,)),
            dma((pieces, n)),
            dma((pieces, n)),
            dma((GROUPS,)),
            dma((slots, n)),
            dma((slots, n)),
            dma((GROUPS,)),
        ],
        compiler_params=pltpu.CompilerParams(
            collective_id=0, has_side_effects=True, vmem_limit_bytes=40 << 20
        ),
        name="filters",
    )(snapshots, table, w)
    modes = pl.pallas_call(
        modes_kernel,
        grid=(GROUPS,),
        out_shape=jax.ShapeDtypeStruct((FREQS, NB, 2, cells), jnp.bfloat16),
        in_specs=[
            pl.BlockSpec((1, 2, NBP, LANES), lambda g: (g, 0, 0, 0)),
            VMEM,
            pl.BlockSpec((2, GROUP, NBP, cells), lambda g: (0, g, 0, 0)),
        ],
        out_specs=pl.BlockSpec((GROUP, NB, 2, cells), lambda g: (g, 0, 0, 0)),
        scratch_shapes=[pltpu.VMEM((2, 2 * LANES, LANES), jnp.float32)],
        compiler_params=pltpu.CompilerParams(vmem_limit_bytes=32 << 20),
        name="modes",
    )(filters, w, wtd)
    return modes.transpose(2, 0, 1, 3)


def solution(mesh):
    return jax.shard_map(
        per_device,
        mesh=mesh,
        in_specs=(P("space", "slab"), P(("slab", "space"))),
        out_specs=P(None, None, None, ("slab", "space")),
        check_vma=False,
    )
```

```python
import functools
import math

import jax
import jax.numpy as jnp
import numpy as np
import ml_dtypes
from jax import lax
from jax.experimental import pallas as pl
from jax.experimental.pallas import tpu as pltpu
from jax.sharding import PartitionSpec as P

SEG = 256
HALF = SEG // 2
NB = 15
FREQS = 129
NBP = 16
GROUP = 8
GROUPS = -(-FREQS // GROUP)
FP = GROUPS * GROUP
LANES = 128
MESH = pl.DeviceIdType.MESH
VMEM = pl.BlockSpec(memory_space=pltpu.VMEM)


def make_table():
    t = np.arange(SEG)
    k = np.arange(FREQS)
    phases = 2.0 * np.pi * (k[:, None] * t[None, :] % SEG) / SEG
    taper = 0.5 - 0.5 * np.cos(2.0 * np.pi * t / SEG)
    scaling = 1.0 / math.sqrt(3.0 * SEG / 8.0)
    table = np.zeros((2, FP, SEG), np.float32)
    table[0, :FREQS] = taper * np.cos(phases) * scaling
    table[1, :FREQS] = -taper * np.sin(phases) * scaling
    return table.reshape(2 * FP, SEG).astype(ml_dtypes.bfloat16)


VLIM = 60
GS = 6
CHUNK = 256


def dft_chunk(tab_ref, x_ref, w_ref, s_ref, h):
    tab = tab_ref[...]
    row_sums = jnp.sum(tab.astype(jnp.float32), axis=1, keepdims=True)
    average = jnp.sum(x_ref[h].astype(jnp.float32), axis=0, keepdims=True) / x_ref.shape[1]
    root = jnp.sqrt(w_ref[:, pl.ds(pl.multiple_of(h * CHUNK, CHUNK), CHUNK)])
    corr = row_sums * (average * root)
    for b in range(NB):
        sp = jnp.dot(tab, x_ref[h, b * HALF : b * HALF + SEG, :], preferred_element_type=jnp.float32)
        sp = sp * root - corr
        for p in range(2):
            for i in range(CHUNK // LANES):
                s_ref[p, i, pl.ds(b, FP, stride=NBP), :] = sp[
                    p * FP : (p + 1) * FP, i * LANES : (i + 1) * LANES
                ]


def gram_group(s_ref, wtd_ref, g_ref, h, g):
    rows = pl.ds(pl.multiple_of(g * LANES, LANES), LANES)
    parts = [
        jnp.concatenate([s_ref[p, i, rows, :] for i in range(CHUNK // LANES)], axis=1).astype(jnp.bfloat16)
        for p in range(2)
    ]
    for p in range(2):
        wtd_ref[h, p, pl.ds(pl.multiple_of(g * GROUP, GROUP), GROUP)] = parts[p].reshape(
            GROUP, NBP, CHUNK
        )
    x = jnp.concatenate(parts, axis=0)
    prod = lax.dot_general(x, x, (((1,), (1,)), ((), ())), preferred_element_type=jnp.float32)
    re = prod[:LANES, :LANES] + prod[LANES:, LANES:]
    im = prod[:LANES, LANES:] - prod[LANES:, :LANES]
    row = lax.broadcasted_iota(jnp.int32, (LANES, LANES), 0) % NBP
    col = lax.broadcasted_iota(jnp.int32, (LANES, LANES), 1) % NBP
    g_ref[g] += fold(jnp.where(row <= col, re, im))


def own_frequency():
    return (
        lax.broadcasted_iota(jnp.int32, (LANES, LANES), 0) // NBP
        == lax.broadcasted_iota(jnp.int32, (LANES, LANES), 1) // NBP
    )


def fold(full):
    freq = lax.broadcasted_iota(jnp.int32, (NBP, LANES), 1) // NBP
    folded = full[:NBP]
    for k in range(1, GROUP):
        folded = jnp.where(freq == k, full[k * NBP : (k + 1) * NBP], folded)
    return folded


def spread(folded):
    return jnp.where(own_frequency(), jnp.concatenate([folded] * GROUP, axis=0), 0.0)


def unpack(packed, swapped, row, col):
    re = jnp.where(row <= col, packed, swapped)
    im = jnp.where(row > col, packed, jnp.where(row < col, -swapped, 0.0))
    return re, im


def group_sum(x, lane):
    for step in (1, 2, 4, 8):
        x = x + jnp.take_along_axis(x, jnp.bitwise_xor(lane, step), axis=1)
    return x


def invert(re, im, real):
    shape = re.shape
    flat = (shape[0] * NBP, LANES)
    row = lax.broadcasted_iota(jnp.int32, (1, NBP, LANES), 1)
    lane = lax.broadcasted_iota(jnp.int32, (1, NBP, LANES), 2)
    col = lane % NBP
    lane_flat = lax.broadcasted_iota(jnp.int32, flat, 1)
    base = lane_flat - lane_flat % NBP
    diag = row == col
    trace = jnp.sum(jnp.where(diag, re, 0.0), axis=1, keepdims=True)
    level = group_sum(jnp.broadcast_to(trace, shape).reshape(flat), lane_flat).reshape(shape) / NB
    level = jnp.where(real, level, 1.0)
    re = re + jnp.where(diag, level, 0.0)
    for j in range(NB):
        index = base + j
        col_re = jnp.take_along_axis(re.reshape(flat), index, axis=1).reshape(shape)
        col_im = jnp.take_along_axis(im.reshape(flat), index, axis=1).reshape(shape)
        inverse = 1.0 / col_re[:, j : j + 1]
        here = (col == j)[:, j : j + 1]
        row_re = jnp.where(here, inverse, re[:, j : j + 1] * inverse)
        row_im = jnp.where(here, 0.0, im[:, j : j + 1] * inverse)
        cross = (row == j) | (col == j)
        col_re = jnp.where(row == j, -1.0, col_re)
        col_im = jnp.where(row == j, 0.0, col_im)
        re = jnp.where(cross, 0.0, re) - (col_re * row_re - col_im * row_im)
        im = jnp.where(cross, 0.0, im) - (col_re * row_im + col_im * row_re)
    return jnp.where(diag, 1.0, 0.0) - level * re, level * im


def filters_kernel(
    n, snap_ref, tab_hbm, w_hbm, wtd_hbm, f_ref,
    tab_ref, w_ref, wtd_ref, own_sem, wtd_sem,
    x_ref, s_ref, g_ref, got_ref, tot_ref,
    x_own, x_send, x_recv, g_send, g_recv, f_send, f_recv,
):
    me = lax.axis_index("space")
    rows = snap_ref.shape[0]
    cells = w_ref.shape[1]
    pieces = cells // CHUNK
    slots = -(-GROUPS // n)

    def peer(i):
        return lax.rem(me + i, n)

    def piece(there, h):
        return snap_ref.at[:, pl.ds(pl.multiple_of(there * cells + h * CHUNK, CHUNK), CHUNK)]

    x_mine = pl.ds(pl.multiple_of(me * rows, rows), rows)

    def local(h):
        return pltpu.make_async_copy(piece(me, h), x_ref.at[h, x_mine], x_own.at[h])

    def write(h):
        cols = pl.ds(pl.multiple_of(h * CHUNK, CHUNK), CHUNK)
        return pltpu.make_async_copy(wtd_ref.at[h], wtd_hbm.at[:, :, :, cols], wtd_sem.at[h])

    def exchange(i, h):
        there = peer(i)
        return pltpu.make_async_remote_copy(
            src_ref=piece(there, h),
            dst_ref=x_ref.at[h, x_mine],
            send_sem=x_send.at[h, i],
            recv_sem=x_recv.at[h, i],
            device_id={"space": there},
            device_id_type=MESH,
        )

    def scatter(g):
        return pltpu.make_async_remote_copy(
            src_ref=g_ref.at[g],
            dst_ref=got_ref.at[g // n, me],
            send_sem=g_send.at[g],
            recv_sem=g_recv.at[g // n, me],
            device_id={"space": lax.rem(g, n)},
            device_id_type=MESH,
        )

    def scattered(slot, source):
        return pltpu.make_async_remote_copy(
            src_ref=g_ref.at[0],
            dst_ref=got_ref.at[slot, source],
            send_sem=g_send.at[0],
            recv_sem=g_recv.at[slot, source],
            device_id={"space": source},
            device_id_type=MESH,
        )

    def gather(g, i):
        return pltpu.make_async_remote_copy(
            src_ref=f_ref.at[g],
            dst_ref=f_ref.at[g],
            send_sem=f_send.at[g // n, i],
            recv_sem=f_recv.at[g],
            device_id={"space": peer(i)},
            device_id_type=MESH,
        )

    barrier = pltpu.get_barrier_semaphore()

    @pl.loop(1, n)
    def _(i):
        pl.semaphore_signal(barrier, inc=1, device_id={"space": peer(i)}, device_id_type=MESH)

    for h in range(pieces):
        local(h).start()
    pl.semaphore_wait(barrier, n - 1)

    @pl.loop(0, pieces)
    def _(h):
        @pl.loop(1, n)
        def _(i):
            exchange(i, h).start()

    constants = (
        pltpu.make_async_copy(tab_hbm, tab_ref, own_sem.at[0]),
        pltpu.make_async_copy(w_hbm, w_ref, own_sem.at[1]),
    )
    for copy in constants:
        copy.start()
    g_ref[...] = jnp.zeros_like(g_ref)
    for p in range(2):
        for i in range(CHUNK // LANES):
            s_ref[p, i, pl.ds(NB, FP, stride=NBP), :] = jnp.zeros((FP, LANES), jnp.float32)

    for copy in constants:
        copy.wait()

    @pl.loop(0, pieces)
    def _(h):
        @pl.loop(1, n)
        def _(i):
            exchange(i, h).wait_recv()

        local(h).wait()
        dft_chunk(tab_ref, x_ref, w_ref, s_ref, h)

        @pl.loop(0, GROUPS, unroll=GROUPS)
        def _(g):
            gram_group(s_ref, wtd_ref, g_ref, h, g)

            @pl.when(jnp.logical_and(h == pieces - 1, lax.rem(g, n) != me))
            def _():
                scatter(g).start()

        write(h).start()

    for slot in range(slots):
        g = slot * n + me

        @pl.when(g < GROUPS)
        def _():
            tot_ref[slot] = g_ref[g]

            @pl.loop(1, n)
            def _(i):
                source = peer(i)
                scattered(slot, source).wait_recv()
                tot_ref[slot] += got_ref[slot, source]

        @pl.when(g >= GROUPS)
        def _():
            tot_ref[slot] = jnp.zeros((NBP, LANES), jnp.float32)

    shape = (slots, NBP, LANES)
    freq = (lax.broadcasted_iota(jnp.int32, shape, 0) * n + me) * GROUP + lax.broadcasted_iota(
        jnp.int32, shape, 2
    ) // NBP
    row = lax.broadcasted_iota(jnp.int32, (1, NBP, LANES), 1)
    col = lax.broadcasted_iota(jnp.int32, (1, NBP, LANES), 2) % NBP
    swapped = jnp.stack([fold(spread(tot_ref[slot]).T) for slot in range(slots)])
    same, other = invert(*unpack(tot_ref[...], swapped, row, col), freq < FREQS)
    filters = jnp.where(row <= col, same, other).astype(jnp.bfloat16)
    for slot in range(slots):
        g = slot * n + me

        @pl.when(g < GROUPS)
        def _():
            f_ref[g] = filters[slot]

            @pl.loop(1, n)
            def _(i):
                gather(g, i).start()

    @pl.loop(0, pieces)
    def _(h):
        @pl.loop(1, n)
        def _(i):
            exchange(i, h).wait_send()

        write(h).wait()

    @pl.loop(0, GROUPS)
    def _(g):
        @pl.when(lax.rem(g, n) != me)
        def _():
            scatter(g).wait_send()
            gather(g, 0).wait_recv()

    for slot in range(slots):
        g = slot * n + me

        @pl.when(g < GROUPS)
        def _():
            @pl.loop(1, n)
            def _(i):
                gather(g, i).wait_send()


def modes_kernel(f_ref, w_ref, wtd_ref, out_ref, mix_ref):
    cells = w_ref.shape[1]
    tiles = cells // LANES
    inverse_root = 1.0 / jnp.sqrt(w_ref[...])
    row = lax.broadcasted_iota(jnp.int32, (LANES, LANES), 0) % NBP
    col = lax.broadcasted_iota(jnp.int32, (LANES, LANES), 1) % NBP
    rows = 2 * tiles * NBP
    for s in range(GS):
        packed = spread(f_ref[s].astype(jnp.float32))
        same, other = unpack(packed, packed.T, row, col)
        filters = jnp.concatenate(
            (jnp.concatenate((same, other), axis=1), jnp.concatenate((-other, same), axis=1)), axis=0
        ).astype(jnp.bfloat16)
        wtd = wtd_ref[:, s * GROUP : (s + 1) * GROUP].reshape(2 * LANES, cells)
        mixed = jnp.dot(filters, wtd, preferred_element_type=jnp.float32) * inverse_root
        for q in range(2):
            for i in range(tiles):
                mix_ref[s, pl.ds(2 * i + q, LANES, stride=2 * tiles), :] = mixed[
                    q * LANES : (q + 1) * LANES, i * LANES : (i + 1) * LANES
                ]
        for k in range(GROUP):
            out_ref[s * GROUP + k] = mix_ref[s, k * rows : k * rows + 2 * tiles * NB, :].astype(jnp.bfloat16)


def per_device(snapshots, weights):
    n = lax.axis_size("space")
    rows = snapshots.shape[0]
    cells = snapshots.shape[1] // n
    pieces = cells // CHUNK
    tiles = cells // LANES
    slots = -(-GROUPS // n)
    table = jnp.asarray(make_table())
    w = weights.reshape(1, cells)
    dma = pltpu.SemaphoreType.DMA
    wtd, filters = pl.pallas_call(
        functools.partial(filters_kernel, n),
        out_shape=(
            jax.ShapeDtypeStruct((2, FP, NBP, cells), jnp.bfloat16),
            jax.ShapeDtypeStruct((GROUPS, NBP, LANES), jnp.bfloat16),
        ),
        in_specs=[pl.BlockSpec(memory_space=pltpu.HBM)] * 3,
        out_specs=(pl.BlockSpec(memory_space=pl.ANY), VMEM),
        scratch_shapes=[
            pltpu.VMEM(table.shape, table.dtype),
            pltpu.VMEM(w.shape, w.dtype),
            pltpu.VMEM((pieces, 2, FP, NBP, CHUNK), jnp.bfloat16),
            dma((2,)),
            dma((pieces,)),
            pltpu.VMEM((pieces, n * rows, CHUNK), jnp.bfloat16),
            pltpu.VMEM((2, CHUNK // LANES, FP * NBP, LANES), jnp.float32),
            pltpu.VMEM((GROUPS, NBP, LANES), jnp.float32),
            pltpu.VMEM((slots, n, NBP, LANES), jnp.float32),
            pltpu.VMEM((slots, NBP, LANES), jnp.float32),
            dma((pieces,)),
            dma((pieces, n)),
            dma((pieces, n)),
            dma((GROUPS,)),
            dma((slots, n)),
            dma((slots, n)),
            dma((GROUPS,)),
        ],
        compiler_params=pltpu.CompilerParams(
            collective_id=0, has_side_effects=True, vmem_limit_bytes=VLIM << 20
        ),
        name="filters",
    )(snapshots, table, w)
    modes = pl.pallas_call(
        modes_kernel,
        grid=(-(-GROUPS // GS),),
        out_shape=jax.ShapeDtypeStruct((FREQS, 2 * tiles * NB, LANES), jnp.bfloat16),
        in_specs=[
            pl.BlockSpec((GS, NBP, LANES), lambda g: (g, 0, 0)),
            VMEM,
            pl.BlockSpec((2, GS * GROUP, NBP, cells), lambda g: (0, g, 0, 0)),
        ],
        out_specs=pl.BlockSpec((GS * GROUP, 2 * tiles * NB, LANES), lambda g: (g, 0, 0)),
        scratch_shapes=[pltpu.VMEM((GS, 2 * tiles * LANES, LANES), jnp.float32)],
        compiler_params=pltpu.CompilerParams(vmem_limit_bytes=VLIM << 20),
        name="modes",
    )(filters, w, wtd)
    modes = modes.reshape(FREQS, NB, tiles, 2, LANES)
    return modes.transpose(3, 0, 1, 2, 4).reshape(2, FREQS, NB, cells)


def solution(mesh):
    return jax.shard_map(
        per_device,
        mesh=mesh,
        in_specs=(P("space", "slab"), P(("slab", "space"))),
        out_specs=P(None, None, None, ("slab", "space")),
        check_vma=False,
    )
```

```python
import functools
import math

import jax
import jax.numpy as jnp
import numpy as np
import ml_dtypes
from jax import lax
from jax.experimental import pallas as pl
from jax.experimental.pallas import tpu as pltpu
from jax.sharding import PartitionSpec as P

SEG = 256
HALF = SEG // 2
NB = 15
FREQS = 129
NBP = 16
GROUP = 8
GROUPS = -(-FREQS // GROUP)
FP = GROUPS * GROUP
LANES = 128
MESH = pl.DeviceIdType.MESH
VMEM = pl.BlockSpec(memory_space=pltpu.VMEM)


def make_table():
    t = np.arange(SEG)
    k = np.arange(FREQS)
    phases = 2.0 * np.pi * (k[:, None] * t[None, :] % SEG) / SEG
    taper = 0.5 - 0.5 * np.cos(2.0 * np.pi * t / SEG)
    scaling = 1.0 / math.sqrt(3.0 * SEG / 8.0)
    table = np.zeros((2, FP, SEG), np.float32)
    table[0, :FREQS] = taper * np.cos(phases) * scaling
    table[1, :FREQS] = -taper * np.sin(phases) * scaling
    return table.reshape(2 * FP, SEG).astype(ml_dtypes.bfloat16)


VLIM = 60
GS = 9
CHUNK = 128


def dft_chunk(tab_ref, x_ref, w_ref, s_ref, h):
    tab = tab_ref[...]
    row_sums = jnp.sum(tab.astype(jnp.float32), axis=1, keepdims=True)
    average = jnp.sum(x_ref[h].astype(jnp.float32), axis=0, keepdims=True) / x_ref.shape[1]
    root = jnp.sqrt(w_ref[:, pl.ds(pl.multiple_of(h * CHUNK, CHUNK), CHUNK)])
    corr = row_sums * (average * root)
    for b in range(NB):
        sp = jnp.dot(tab, x_ref[h, b * HALF : b * HALF + SEG, :], preferred_element_type=jnp.float32)
        sp = sp * root - corr
        for p in range(2):
            for i in range(CHUNK // LANES):
                s_ref[p, i, pl.ds(b, FP, stride=NBP), :] = sp[
                    p * FP : (p + 1) * FP, i * LANES : (i + 1) * LANES
                ]


def gram_group(s_ref, wtd_ref, g_ref, h, g):
    rows = pl.ds(pl.multiple_of(g * LANES, LANES), LANES)
    parts = [
        jnp.concatenate([s_ref[p, i, rows, :] for i in range(CHUNK // LANES)], axis=1).astype(jnp.bfloat16)
        for p in range(2)
    ]
    for p in range(2):
        wtd_ref[h, p, pl.ds(pl.multiple_of(g * GROUP, GROUP), GROUP)] = parts[p].reshape(
            GROUP, NBP, CHUNK
        )
    x = jnp.concatenate(parts, axis=0)
    prod = lax.dot_general(x, x, (((1,), (1,)), ((), ())), preferred_element_type=jnp.float32)
    re = prod[:LANES, :LANES] + prod[LANES:, LANES:]
    im = prod[:LANES, LANES:] - prod[LANES:, :LANES]
    row = lax.broadcasted_iota(jnp.int32, (LANES, LANES), 0) % NBP
    col = lax.broadcasted_iota(jnp.int32, (LANES, LANES), 1) % NBP
    g_ref[g] += fold(jnp.where(row <= col, re, im))


def own_frequency():
    return (
        lax.broadcasted_iota(jnp.int32, (LANES, LANES), 0) // NBP
        == lax.broadcasted_iota(jnp.int32, (LANES, LANES), 1) // NBP
    )


def fold(full):
    freq = lax.broadcasted_iota(jnp.int32, (NBP, LANES), 1) // NBP
    folded = full[:NBP]
    for k in range(1, GROUP):
        folded = jnp.where(freq == k, full[k * NBP : (k + 1) * NBP], folded)
    return folded


def spread(folded):
    return jnp.where(own_frequency(), jnp.concatenate([folded] * GROUP, axis=0), 0.0)


def unpack(packed, swapped, row, col):
    re = jnp.where(row <= col, packed, swapped)
    im = jnp.where(row > col, packed, jnp.where(row < col, -swapped, 0.0))
    return re, im


def group_sum(x, lane):
    for step in (1, 2, 4, 8):
        x = x + jnp.take_along_axis(x, jnp.bitwise_xor(lane, step), axis=1)
    return x


def invert(re, im, real):
    shape = re.shape
    flat = (shape[0] * NBP, LANES)
    row = lax.broadcasted_iota(jnp.int32, (1, NBP, LANES), 1)
    lane = lax.broadcasted_iota(jnp.int32, (1, NBP, LANES), 2)
    col = lane % NBP
    lane_flat = lax.broadcasted_iota(jnp.int32, flat, 1)
    base = lane_flat - lane_flat % NBP
    diag = row == col
    trace = jnp.sum(jnp.where(diag, re, 0.0), axis=1, keepdims=True)
    level = group_sum(jnp.broadcast_to(trace, shape).reshape(flat), lane_flat).reshape(shape) / NB
    level = jnp.where(real, level, 1.0)
    re = re + jnp.where(diag, level, 0.0)
    for j in range(NB):
        index = base + j
        col_re = jnp.take_along_axis(re.reshape(flat), index, axis=1).reshape(shape)
        col_im = jnp.take_along_axis(im.reshape(flat), index, axis=1).reshape(shape)
        inverse = 1.0 / col_re[:, j : j + 1]
        here = (col == j)[:, j : j + 1]
        row_re = jnp.where(here, inverse, re[:, j : j + 1] * inverse)
        row_im = jnp.where(here, 0.0, im[:, j : j + 1] * inverse)
        cross = (row == j) | (col == j)
        col_re = jnp.where(row == j, -1.0, col_re)
        col_im = jnp.where(row == j, 0.0, col_im)
        re = jnp.where(cross, 0.0, re) - (col_re * row_re - col_im * row_im)
        im = jnp.where(cross, 0.0, im) - (col_re * row_im + col_im * row_re)
    return jnp.where(diag, 1.0, 0.0) - level * re, level * im


def filters_kernel(
    n, snap_ref, tab_hbm, w_hbm, wtd_hbm, f_ref,
    tab_ref, w_ref, wtd_ref, own_sem, wtd_sem,
    x_ref, s_ref, g_ref, got_ref, tot_ref,
    x_own, x_send, x_recv, g_send, g_recv, f_send, f_recv,
):
    me = lax.axis_index("space")
    rows = snap_ref.shape[0]
    cells = w_ref.shape[1]
    pieces = cells // CHUNK
    slots = -(-GROUPS // n)

    def peer(i):
        return lax.rem(me + i, n)

    def piece(there, h):
        return snap_ref.at[:, pl.ds(pl.multiple_of(there * cells + h * CHUNK, CHUNK), CHUNK)]

    x_mine = pl.ds(pl.multiple_of(me * rows, rows), rows)

    def local(h):
        return pltpu.make_async_copy(piece(me, h), x_ref.at[h, x_mine], x_own.at[h])

    def write(h):
        cols = pl.ds(pl.multiple_of(h * CHUNK, CHUNK), CHUNK)
        return pltpu.make_async_copy(wtd_ref.at[h], wtd_hbm.at[:, :, :, cols], wtd_sem.at[h])

    def exchange(i, h):
        there = peer(i)
        return pltpu.make_async_remote_copy(
            src_ref=piece(there, h),
            dst_ref=x_ref.at[h, x_mine],
            send_sem=x_send.at[h, i],
            recv_sem=x_recv.at[h, i],
            device_id={"space": there},
            device_id_type=MESH,
        )

    def scatter(g):
        return pltpu.make_async_remote_copy(
            src_ref=g_ref.at[g],
            dst_ref=got_ref.at[g // n, me],
            send_sem=g_send.at[g],
            recv_sem=g_recv.at[g // n, me],
            device_id={"space": lax.rem(g, n)},
            device_id_type=MESH,
        )

    def scattered(slot, source):
        return pltpu.make_async_remote_copy(
            src_ref=g_ref.at[0],
            dst_ref=got_ref.at[slot, source],
            send_sem=g_send.at[0],
            recv_sem=g_recv.at[slot, source],
            device_id={"space": source},
            device_id_type=MESH,
        )

    def gather(g, i):
        return pltpu.make_async_remote_copy(
            src_ref=f_ref.at[g],
            dst_ref=f_ref.at[g],
            send_sem=f_send.at[g // n, i],
            recv_sem=f_recv.at[g],
            device_id={"space": peer(i)},
            device_id_type=MESH,
        )

    barrier = pltpu.get_barrier_semaphore()

    @pl.loop(1, n)
    def _(i):
        pl.semaphore_signal(barrier, inc=1, device_id={"space": peer(i)}, device_id_type=MESH)

    for h in range(pieces):
        local(h).start()
    pl.semaphore_wait(barrier, n - 1)

    @pl.loop(0, pieces)
    def _(h):
        @pl.loop(1, n)
        def _(i):
            exchange(i, h).start()

    constants = (
        pltpu.make_async_copy(tab_hbm, tab_ref, own_sem.at[0]),
        pltpu.make_async_copy(w_hbm, w_ref, own_sem.at[1]),
    )
    for copy in constants:
        copy.start()
    g_ref[...] = jnp.zeros_like(g_ref)
    for p in range(2):
        for i in range(CHUNK // LANES):
            s_ref[p, i, pl.ds(NB, FP, stride=NBP), :] = jnp.zeros((FP, LANES), jnp.float32)

    for copy in constants:
        copy.wait()

    @pl.loop(0, pieces)
    def _(h):
        @pl.loop(1, n)
        def _(i):
            exchange(i, h).wait_recv()

        local(h).wait()
        dft_chunk(tab_ref, x_ref, w_ref, s_ref, h)

        @pl.loop(0, GROUPS, unroll=GROUPS)
        def _(g):
            gram_group(s_ref, wtd_ref, g_ref, h, g)

        write(h).start()

    @pl.loop(0, GROUPS)
    def _(g):
        @pl.when(lax.rem(g, n) != me)
        def _():
            scatter(g).start()

    for slot in range(slots):
        g = slot * n + me

        @pl.when(g < GROUPS)
        def _():
            tot_ref[slot] = g_ref[g]

            @pl.loop(1, n)
            def _(i):
                source = peer(i)
                scattered(slot, source).wait_recv()
                tot_ref[slot] += got_ref[slot, source]

        @pl.when(g >= GROUPS)
        def _():
            tot_ref[slot] = jnp.zeros((NBP, LANES), jnp.float32)

    shape = (slots, NBP, LANES)
    freq = (lax.broadcasted_iota(jnp.int32, shape, 0) * n + me) * GROUP + lax.broadcasted_iota(
        jnp.int32, shape, 2
    ) // NBP
    row = lax.broadcasted_iota(jnp.int32, (1, NBP, LANES), 1)
    col = lax.broadcasted_iota(jnp.int32, (1, NBP, LANES), 2) % NBP
    swapped = jnp.stack([fold(spread(tot_ref[slot]).T) for slot in range(slots)])
    same, other = invert(*unpack(tot_ref[...], swapped, row, col), freq < FREQS)
    filters = jnp.where(row <= col, same, other).astype(jnp.bfloat16)
    for slot in range(slots):
        g = slot * n + me

        @pl.when(g < GROUPS)
        def _():
            f_ref[g] = filters[slot]

            @pl.loop(1, n)
            def _(i):
                gather(g, i).start()

    @pl.loop(0, pieces)
    def _(h):
        @pl.loop(1, n)
        def _(i):
            exchange(i, h).wait_send()

        write(h).wait()

    @pl.loop(0, GROUPS)
    def _(g):
        @pl.when(lax.rem(g, n) != me)
        def _():
            scatter(g).wait_send()
            gather(g, 0).wait_recv()

    for slot in range(slots):
        g = slot * n + me

        @pl.when(g < GROUPS)
        def _():
            @pl.loop(1, n)
            def _(i):
                gather(g, i).wait_send()


def modes_kernel(f_ref, w_ref, wtd_ref, out_ref, mix_ref):
    cells = w_ref.shape[1]
    tiles = cells // LANES
    inverse_root = 1.0 / jnp.sqrt(w_ref[...])
    row = lax.broadcasted_iota(jnp.int32, (LANES, LANES), 0) % NBP
    col = lax.broadcasted_iota(jnp.int32, (LANES, LANES), 1) % NBP
    rows = 2 * tiles * NBP
    for s in range(GS):
        packed = spread(f_ref[s].astype(jnp.float32))
        same, other = unpack(packed, packed.T, row, col)
        filters = jnp.concatenate(
            (jnp.concatenate((same, other), axis=1), jnp.concatenate((-other, same), axis=1)), axis=0
        ).astype(jnp.bfloat16)
        wtd = wtd_ref[:, s * GROUP : (s + 1) * GROUP].reshape(2 * LANES, cells)
        mixed = jnp.dot(filters, wtd, preferred_element_type=jnp.float32) * inverse_root
        for q in range(2):
            for i in range(tiles):
                mix_ref[s, pl.ds(2 * i + q, LANES, stride=2 * tiles), :] = mixed[
                    q * LANES : (q + 1) * LANES, i * LANES : (i + 1) * LANES
                ]
        for k in range(GROUP):
            out_ref[s * GROUP + k] = mix_ref[s, k * rows : k * rows + 2 * tiles * NB, :].astype(jnp.bfloat16)


def per_device(snapshots, weights):
    n = lax.axis_size("space")
    rows = snapshots.shape[0]
    cells = snapshots.shape[1] // n
    pieces = cells // CHUNK
    tiles = cells // LANES
    slots = -(-GROUPS // n)
    table = jnp.asarray(make_table())
    w = weights.reshape(1, cells)
    dma = pltpu.SemaphoreType.DMA
    wtd, filters = pl.pallas_call(
        functools.partial(filters_kernel, n),
        out_shape=(
            jax.ShapeDtypeStruct((2, FP, NBP, cells), jnp.bfloat16),
            jax.ShapeDtypeStruct((GROUPS, NBP, LANES), jnp.bfloat16),
        ),
        in_specs=[pl.BlockSpec(memory_space=pltpu.HBM)] * 3,
        out_specs=(pl.BlockSpec(memory_space=pl.ANY), VMEM),
        scratch_shapes=[
            pltpu.VMEM(table.shape, table.dtype),
            pltpu.VMEM(w.shape, w.dtype),
            pltpu.VMEM((pieces, 2, FP, NBP, CHUNK), jnp.bfloat16),
            dma((2,)),
            dma((pieces,)),
            pltpu.VMEM((pieces, n * rows, CHUNK), jnp.bfloat16),
            pltpu.VMEM((2, CHUNK // LANES, FP * NBP, LANES), jnp.float32),
            pltpu.VMEM((GROUPS, NBP, LANES), jnp.float32),
            pltpu.VMEM((slots, n, NBP, LANES), jnp.float32),
            pltpu.VMEM((slots, NBP, LANES), jnp.float32),
            dma((pieces,)),
            dma((pieces, n)),
            dma((pieces, n)),
            dma((GROUPS,)),
            dma((slots, n)),
            dma((slots, n)),
            dma((GROUPS,)),
        ],
        compiler_params=pltpu.CompilerParams(
            collective_id=0, has_side_effects=True, vmem_limit_bytes=VLIM << 20
        ),
        name="filters",
    )(snapshots, table, w)
    modes = pl.pallas_call(
        modes_kernel,
        grid=(-(-GROUPS // GS),),
        out_shape=jax.ShapeDtypeStruct((FREQS, 2 * tiles * NB, LANES), jnp.bfloat16),
        in_specs=[
            pl.BlockSpec((GS, NBP, LANES), lambda g: (g, 0, 0)),
            VMEM,
            pl.BlockSpec((2, GS * GROUP, NBP, cells), lambda g: (0, g, 0, 0)),
        ],
        out_specs=pl.BlockSpec((GS * GROUP, 2 * tiles * NB, LANES), lambda g: (g, 0, 0)),
        scratch_shapes=[pltpu.VMEM((GS, 2 * tiles * LANES, LANES), jnp.float32)],
        compiler_params=pltpu.CompilerParams(vmem_limit_bytes=VLIM << 20),
        name="modes",
    )(filters, w, wtd)
    modes = modes.reshape(FREQS, NB, tiles, 2, LANES)
    return modes.transpose(3, 0, 1, 2, 4).reshape(2, FREQS, NB, cells)


def solution(mesh):
    return jax.shard_map(
        per_device,
        mesh=mesh,
        in_specs=(P("space", "slab"), P(("slab", "space"))),
        out_specs=P(None, None, None, ("slab", "space")),
        check_vma=False,
    )
```

```python
import functools
import math

import jax
import jax.numpy as jnp
import numpy as np
import ml_dtypes
from jax import lax
from jax.experimental import pallas as pl
from jax.experimental.pallas import tpu as pltpu
from jax.sharding import PartitionSpec as P

SEG = 256
HALF = SEG // 2
NB = 15
FREQS = 129
NBP = 16
GROUP = 8
GROUPS = -(-FREQS // GROUP)
FP = GROUPS * GROUP
LANES = 128
MESH = pl.DeviceIdType.MESH
VMEM = pl.BlockSpec(memory_space=pltpu.VMEM)


def make_table():
    t = np.arange(SEG)
    k = np.arange(FREQS)
    phases = 2.0 * np.pi * (k[:, None] * t[None, :] % SEG) / SEG
    taper = 0.5 - 0.5 * np.cos(2.0 * np.pi * t / SEG)
    scaling = 1.0 / math.sqrt(3.0 * SEG / 8.0)
    table = np.zeros((2, FP, SEG), np.float32)
    table[0, :FREQS] = taper * np.cos(phases) * scaling
    table[1, :FREQS] = -taper * np.sin(phases) * scaling
    return table.reshape(2 * FP, SEG).astype(ml_dtypes.bfloat16)


VLIM = 60
GS = 9
CHUNK = 128


def dft_chunk(tab_ref, x_ref, w_ref, s_ref, h):
    tab = tab_ref[...]
    row_sums = jnp.sum(tab.astype(jnp.float32), axis=1, keepdims=True)
    average = jnp.sum(x_ref[h].astype(jnp.float32), axis=0, keepdims=True) / x_ref.shape[1]
    root = jnp.sqrt(w_ref[:, pl.ds(pl.multiple_of(h * CHUNK, CHUNK), CHUNK)])
    corr = row_sums * (average * root)
    for b in range(NB):
        sp = jnp.dot(tab, x_ref[h, b * HALF : b * HALF + SEG, :], preferred_element_type=jnp.float32)
        sp = sp * root - corr
        for p in range(2):
            for i in range(CHUNK // LANES):
                s_ref[p, i, pl.ds(b, FP, stride=NBP), :] = sp[
                    p * FP : (p + 1) * FP, i * LANES : (i + 1) * LANES
                ]


def gram_group(s_ref, wtd_ref, g_ref, h, g):
    rows = pl.ds(pl.multiple_of(g * LANES, LANES), LANES)
    parts = [
        jnp.concatenate([s_ref[p, i, rows, :] for i in range(CHUNK // LANES)], axis=1).astype(jnp.bfloat16)
        for p in range(2)
    ]
    for p in range(2):
        wtd_ref[h, p, pl.ds(pl.multiple_of(g * GROUP, GROUP), GROUP)] = parts[p].reshape(
            GROUP, NBP, CHUNK
        )
    x = jnp.concatenate(parts, axis=0)
    prod = lax.dot_general(x, x, (((1,), (1,)), ((), ())), preferred_element_type=jnp.float32)
    re = prod[:LANES, :LANES] + prod[LANES:, LANES:]
    im = prod[:LANES, LANES:] - prod[LANES:, :LANES]
    row = lax.broadcasted_iota(jnp.int32, (LANES, LANES), 0) % NBP
    col = lax.broadcasted_iota(jnp.int32, (LANES, LANES), 1) % NBP
    g_ref[g] += fold(jnp.where(row <= col, re, im))


def own_frequency():
    return (
        lax.broadcasted_iota(jnp.int32, (LANES, LANES), 0) // NBP
        == lax.broadcasted_iota(jnp.int32, (LANES, LANES), 1) // NBP
    )


def fold(full):
    freq = lax.broadcasted_iota(jnp.int32, (NBP, LANES), 1) // NBP
    folded = full[:NBP]
    for k in range(1, GROUP):
        folded = jnp.where(freq == k, full[k * NBP : (k + 1) * NBP], folded)
    return folded


def spread(folded):
    return jnp.where(own_frequency(), jnp.concatenate([folded] * GROUP, axis=0), 0.0)


def unpack(packed, swapped, row, col):
    re = jnp.where(row <= col, packed, swapped)
    im = jnp.where(row > col, packed, jnp.where(row < col, -swapped, 0.0))
    return re, im


def group_sum(x, lane):
    for step in (1, 2, 4, 8):
        x = x + jnp.take_along_axis(x, jnp.bitwise_xor(lane, step), axis=1)
    return x


def invert(re, im, real):
    shape = re.shape
    flat = (shape[0] * NBP, LANES)
    row = lax.broadcasted_iota(jnp.int32, (1, NBP, LANES), 1)
    lane = lax.broadcasted_iota(jnp.int32, (1, NBP, LANES), 2)
    col = lane % NBP
    lane_flat = lax.broadcasted_iota(jnp.int32, flat, 1)
    base = lane_flat - lane_flat % NBP
    diag = row == col
    trace = jnp.sum(jnp.where(diag, re, 0.0), axis=1, keepdims=True)
    level = group_sum(jnp.broadcast_to(trace, shape).reshape(flat), lane_flat).reshape(shape) / NB
    level = jnp.where(real, level, 1.0)
    re = re + jnp.where(diag, level, 0.0)
    for j in range(NB):
        index = base + j
        col_re = jnp.take_along_axis(re.reshape(flat), index, axis=1).reshape(shape)
        col_im = jnp.take_along_axis(im.reshape(flat), index, axis=1).reshape(shape)
        inverse = 1.0 / col_re[:, j : j + 1]
        here = (col == j)[:, j : j + 1]
        row_re = jnp.where(here, inverse, re[:, j : j + 1] * inverse)
        row_im = jnp.where(here, 0.0, im[:, j : j + 1] * inverse)
        cross = (row == j) | (col == j)
        col_re = jnp.where(row == j, -1.0, col_re)
        col_im = jnp.where(row == j, 0.0, col_im)
        re = jnp.where(cross, 0.0, re) - (col_re * row_re - col_im * row_im)
        im = jnp.where(cross, 0.0, im) - (col_re * row_im + col_im * row_re)
    return jnp.where(diag, 1.0, 0.0) - level * re, level * im


def filters_kernel(
    n, snap_ref, tab_hbm, w_hbm, wtd_hbm, f_hbm,
    tab_ref, w_ref, wtd_ref, f_ref, own_sem, wtd_sem, f_own,
    x_ref, s_ref, g_ref, got_ref, tot_ref,
    x_own, x_send, x_recv, g_send, g_recv, f_send, f_recv,
):
    me = lax.axis_index("space")
    rows = snap_ref.shape[0]
    cells = w_ref.shape[1]
    pieces = cells // CHUNK
    slots = -(-GROUPS // n)

    def peer(i):
        return lax.rem(me + i, n)

    def piece(there, h):
        return snap_ref.at[:, pl.ds(pl.multiple_of(there * cells + h * CHUNK, CHUNK), CHUNK)]

    x_mine = pl.ds(pl.multiple_of(me * rows, rows), rows)

    def local(h):
        return pltpu.make_async_copy(piece(me, h), x_ref.at[h, x_mine], x_own.at[h])

    def write(h):
        cols = pl.ds(pl.multiple_of(h * CHUNK, CHUNK), CHUNK)
        return pltpu.make_async_copy(wtd_ref.at[h], wtd_hbm.at[:, :, :, cols], wtd_sem.at[h])

    def exchange(i, h):
        there = peer((n + 1) // 2 + jnp.where(i % 2 == 1, (i - 1) // 2, -(i // 2)))
        return pltpu.make_async_remote_copy(
            src_ref=piece(there, h),
            dst_ref=x_ref.at[h, x_mine],
            send_sem=x_send.at[h, i],
            recv_sem=x_recv.at[h, i],
            device_id={"space": there},
            device_id_type=MESH,
        )

    def scatter(g):
        return pltpu.make_async_remote_copy(
            src_ref=g_ref.at[g],
            dst_ref=got_ref.at[g // n, me],
            send_sem=g_send.at[g],
            recv_sem=g_recv.at[g // n, me],
            device_id={"space": lax.rem(g, n)},
            device_id_type=MESH,
        )

    def scattered(slot, source):
        return pltpu.make_async_remote_copy(
            src_ref=g_ref.at[0],
            dst_ref=got_ref.at[slot, source],
            send_sem=g_send.at[0],
            recv_sem=g_recv.at[slot, source],
            device_id={"space": source},
            device_id_type=MESH,
        )

    def keep(slot):
        return pltpu.make_async_copy(f_ref.at[slot], f_hbm.at[slot * n + me], f_own.at[slot])

    def gather(g, i):
        return pltpu.make_async_remote_copy(
            src_ref=f_ref.at[g // n],
            dst_ref=f_hbm.at[g],
            send_sem=f_send.at[g // n, i],
            recv_sem=f_recv.at[g],
            device_id={"space": peer(i)},
            device_id_type=MESH,
        )

    barrier = pltpu.get_barrier_semaphore()

    @pl.loop(1, n)
    def _(i):
        pl.semaphore_signal(barrier, inc=1, device_id={"space": peer(i)}, device_id_type=MESH)

    for h in range(pieces):
        local(h).start()
    pl.semaphore_wait(barrier, n - 1)

    @pl.loop(0, pieces)
    def _(h):
        @pl.loop(1, n)
        def _(i):
            exchange(i, h).start()

    constants = (
        pltpu.make_async_copy(tab_hbm, tab_ref, own_sem.at[0]),
        pltpu.make_async_copy(w_hbm, w_ref, own_sem.at[1]),
    )
    for copy in constants:
        copy.start()
    g_ref[...] = jnp.zeros_like(g_ref)
    for p in range(2):
        for i in range(CHUNK // LANES):
            s_ref[p, i, pl.ds(NB, FP, stride=NBP), :] = jnp.zeros((FP, LANES), jnp.float32)

    for copy in constants:
        copy.wait()

    @pl.loop(0, pieces)
    def _(h):
        @pl.loop(1, n)
        def _(i):
            exchange(i, h).wait_recv()

        local(h).wait()
        dft_chunk(tab_ref, x_ref, w_ref, s_ref, h)

        @pl.loop(0, GROUPS, unroll=GROUPS)
        def _(g):
            gram_group(s_ref, wtd_ref, g_ref, h, g)

        write(h).start()

    @pl.loop(0, GROUPS)
    def _(g):
        @pl.when(lax.rem(g, n) != me)
        def _():
            scatter(g).start()

    for slot in range(slots):
        g = slot * n + me

        @pl.when(g < GROUPS)
        def _():
            tot_ref[slot] = g_ref[g]

            @pl.loop(1, n)
            def _(i):
                source = peer(i)
                scattered(slot, source).wait_recv()
                tot_ref[slot] += got_ref[slot, source]

        @pl.when(g >= GROUPS)
        def _():
            tot_ref[slot] = jnp.zeros((NBP, LANES), jnp.float32)

    shape = (slots, NBP, LANES)
    freq = (lax.broadcasted_iota(jnp.int32, shape, 0) * n + me) * GROUP + lax.broadcasted_iota(
        jnp.int32, shape, 2
    ) // NBP
    row = lax.broadcasted_iota(jnp.int32, (1, NBP, LANES), 1)
    col = lax.broadcasted_iota(jnp.int32, (1, NBP, LANES), 2) % NBP
    swapped = jnp.stack([fold(spread(tot_ref[slot]).T) for slot in range(slots)])
    same, other = invert(*unpack(tot_ref[...], swapped, row, col), freq < FREQS)
    filters = jnp.where(row <= col, same, other).astype(jnp.bfloat16)
    for slot in range(slots):
        g = slot * n + me

        @pl.when(g < GROUPS)
        def _():
            f_ref[slot] = filters[slot]
            keep(slot).start()

            @pl.loop(1, n)
            def _(i):
                gather(g, i).start()

    @pl.loop(0, pieces)
    def _(h):
        @pl.loop(1, n)
        def _(i):
            exchange(i, h).wait_send()

        write(h).wait()

    @pl.loop(0, GROUPS)
    def _(g):
        @pl.when(lax.rem(g, n) != me)
        def _():
            scatter(g).wait_send()
            gather(g, 0).wait_recv()

    for slot in range(slots):
        g = slot * n + me

        @pl.when(g < GROUPS)
        def _():
            @pl.loop(1, n)
            def _(i):
                gather(g, i).wait_send()

            keep(slot).wait()


def modes_kernel(f_ref, w_ref, wtd_ref, out_ref, mix_ref):
    cells = w_ref.shape[1]
    tiles = cells // LANES
    inverse_root = 1.0 / jnp.sqrt(w_ref[...])
    row = lax.broadcasted_iota(jnp.int32, (LANES, LANES), 0) % NBP
    col = lax.broadcasted_iota(jnp.int32, (LANES, LANES), 1) % NBP
    rows = 2 * tiles * NBP
    for s in range(GS):
        packed = spread(f_ref[s].astype(jnp.float32))
        same, other = unpack(packed, packed.T, row, col)
        filters = jnp.concatenate(
            (jnp.concatenate((same, other), axis=1), jnp.concatenate((-other, same), axis=1)), axis=0
        ).astype(jnp.bfloat16)
        wtd = wtd_ref[:, s * GROUP : (s + 1) * GROUP].reshape(2 * LANES, cells)
        mixed = jnp.dot(filters, wtd, preferred_element_type=jnp.float32) * inverse_root
        for q in range(2):
            for i in range(tiles):
                mix_ref[s, pl.ds(2 * i + q, LANES, stride=2 * tiles), :] = mixed[
                    q * LANES : (q + 1) * LANES, i * LANES : (i + 1) * LANES
                ]
        for k in range(GROUP):
            out_ref[s * GROUP + k] = mix_ref[s, k * rows : k * rows + 2 * tiles * NB, :].astype(jnp.bfloat16)


def per_device(snapshots, weights):
    n = lax.axis_size("space")
    rows = snapshots.shape[0]
    cells = snapshots.shape[1] // n
    pieces = cells // CHUNK
    tiles = cells // LANES
    slots = -(-GROUPS // n)
    table = jnp.asarray(make_table())
    w = weights.reshape(1, cells)
    dma = pltpu.SemaphoreType.DMA
    wtd, filters = pl.pallas_call(
        functools.partial(filters_kernel, n),
        out_shape=(
            jax.ShapeDtypeStruct((2, FP, NBP, cells), jnp.bfloat16),
            jax.ShapeDtypeStruct((GROUPS, NBP, LANES), jnp.bfloat16),
        ),
        in_specs=[pl.BlockSpec(memory_space=pltpu.HBM)] * 3,
        out_specs=(pl.BlockSpec(memory_space=pl.ANY),) * 2,
        scratch_shapes=[
            pltpu.VMEM(table.shape, table.dtype),
            pltpu.VMEM(w.shape, w.dtype),
            pltpu.VMEM((pieces, 2, FP, NBP, CHUNK), jnp.bfloat16),
            pltpu.VMEM((slots, NBP, LANES), jnp.bfloat16),
            dma((2,)),
            dma((pieces,)),
            dma((slots,)),
            pltpu.VMEM((pieces, n * rows, CHUNK), jnp.bfloat16),
            pltpu.VMEM((2, CHUNK // LANES, FP * NBP, LANES), jnp.float32),
            pltpu.VMEM((GROUPS, NBP, LANES), jnp.float32),
            pltpu.VMEM((slots, n, NBP, LANES), jnp.float32),
            pltpu.VMEM((slots, NBP, LANES), jnp.float32),
            dma((pieces,)),
            dma((pieces, n)),
            dma((pieces, n)),
            dma((GROUPS,)),
            dma((slots, n)),
            dma((slots, n)),
            dma((GROUPS,)),
        ],
        compiler_params=pltpu.CompilerParams(
            collective_id=0, has_side_effects=True, vmem_limit_bytes=VLIM << 20
        ),
        name="filters",
    )(snapshots, table, w)
    modes = pl.pallas_call(
        modes_kernel,
        grid=(-(-GROUPS // GS),),
        out_shape=jax.ShapeDtypeStruct((FREQS, 2 * tiles * NB, LANES), jnp.bfloat16),
        in_specs=[
            pl.BlockSpec((GS, NBP, LANES), lambda g: (g, 0, 0)),
            VMEM,
            pl.BlockSpec((2, GS * GROUP, NBP, cells), lambda g: (0, g, 0, 0)),
        ],
        out_specs=pl.BlockSpec((GS * GROUP, 2 * tiles * NB, LANES), lambda g: (g, 0, 0)),
        scratch_shapes=[pltpu.VMEM((GS, 2 * tiles * LANES, LANES), jnp.float32)],
        compiler_params=pltpu.CompilerParams(vmem_limit_bytes=VLIM << 20),
        name="modes",
    )(filters, w, wtd)
    modes = modes.reshape(FREQS, NB, tiles, 2, LANES)
    return modes.transpose(3, 0, 1, 2, 4).reshape(2, FREQS, NB, cells)


def solution(mesh):
    return jax.shard_map(
        per_device,
        mesh=mesh,
        in_specs=(P("space", "slab"), P(("slab", "space"))),
        out_specs=P(None, None, None, ("slab", "space")),
        check_vma=False,
    )
```

```python
import functools
import math

import jax
import jax.numpy as jnp
import numpy as np
import ml_dtypes
from jax import lax
from jax.experimental import pallas as pl
from jax.experimental.pallas import tpu as pltpu
from jax.sharding import PartitionSpec as P

SEG = 256
HALF = SEG // 2
NB = 15
FREQS = 129
NBP = 16
GROUP = 8
GROUPS = -(-FREQS // GROUP)
FP = GROUPS * GROUP
LANES = 128
MESH = pl.DeviceIdType.MESH
VMEM = pl.BlockSpec(memory_space=pltpu.VMEM)


def make_table():
    t = np.arange(SEG)
    k = np.arange(FREQS)
    phases = 2.0 * np.pi * (k[:, None] * t[None, :] % SEG) / SEG
    taper = 0.5 - 0.5 * np.cos(2.0 * np.pi * t / SEG)
    scaling = 1.0 / math.sqrt(3.0 * SEG / 8.0)
    table = np.zeros((2, FP, SEG), np.float32)
    table[0, :FREQS] = taper * np.cos(phases) * scaling
    table[1, :FREQS] = -taper * np.sin(phases) * scaling
    return table.reshape(2 * FP, SEG).astype(ml_dtypes.bfloat16)


VLIM = 60
GS = 9
CHUNK = 128


def dft_chunk(tab_ref, x_ref, w_ref, s_ref, h):
    tab = tab_ref[...]
    row_sums = jnp.sum(tab.astype(jnp.float32), axis=1, keepdims=True)
    average = jnp.sum(x_ref[h].astype(jnp.float32), axis=0, keepdims=True) / x_ref.shape[1]
    root = jnp.sqrt(w_ref[:, pl.ds(pl.multiple_of(h * CHUNK, CHUNK), CHUNK)])
    corr = row_sums * (average * root)
    for b in range(NB):
        sp = jnp.dot(tab, x_ref[h, b * HALF : b * HALF + SEG, :], preferred_element_type=jnp.float32)
        sp = sp * root - corr
        for p in range(2):
            for i in range(CHUNK // LANES):
                s_ref[p, i, pl.ds(b, FP, stride=NBP), :] = sp[
                    p * FP : (p + 1) * FP, i * LANES : (i + 1) * LANES
                ]


def gram_group(s_ref, wtd_ref, g_ref, h, g):
    rows = pl.ds(pl.multiple_of(g * LANES, LANES), LANES)
    parts = [
        jnp.concatenate([s_ref[p, i, rows, :] for i in range(CHUNK // LANES)], axis=1).astype(jnp.bfloat16)
        for p in range(2)
    ]
    for p in range(2):
        wtd_ref[h, p, pl.ds(pl.multiple_of(g * GROUP, GROUP), GROUP)] = parts[p].reshape(
            GROUP, NBP, CHUNK
        )
    x = jnp.concatenate(parts, axis=0)
    prod = lax.dot_general(x, x, (((1,), (1,)), ((), ())), preferred_element_type=jnp.float32)
    re = prod[:LANES, :LANES] + prod[LANES:, LANES:]
    im = prod[:LANES, LANES:] - prod[LANES:, :LANES]
    row = lax.broadcasted_iota(jnp.int32, (LANES, LANES), 0) % NBP
    col = lax.broadcasted_iota(jnp.int32, (LANES, LANES), 1) % NBP
    g_ref[g] += fold(jnp.where(row <= col, re, im))


def own_frequency():
    return (
        lax.broadcasted_iota(jnp.int32, (LANES, LANES), 0) // NBP
        == lax.broadcasted_iota(jnp.int32, (LANES, LANES), 1) // NBP
    )


def fold(full):
    freq = lax.broadcasted_iota(jnp.int32, (NBP, LANES), 1) // NBP
    folded = full[:NBP]
    for k in range(1, GROUP):
        folded = jnp.where(freq == k, full[k * NBP : (k + 1) * NBP], folded)
    return folded


def spread(folded):
    return jnp.where(own_frequency(), jnp.concatenate([folded] * GROUP, axis=0), 0.0)


def unpack(packed, swapped, row, col):
    re = jnp.where(row <= col, packed, swapped)
    im = jnp.where(row > col, packed, jnp.where(row < col, -swapped, 0.0))
    return re, im


def group_sum(x, lane):
    for step in (1, 2, 4, 8):
        x = x + jnp.take_along_axis(x, jnp.bitwise_xor(lane, step), axis=1)
    return x


def invert(re, im, real):
    shape = re.shape
    flat = (shape[0] * NBP, LANES)
    row = lax.broadcasted_iota(jnp.int32, (1, NBP, LANES), 1)
    lane = lax.broadcasted_iota(jnp.int32, (1, NBP, LANES), 2)
    col = lane % NBP
    lane_flat = lax.broadcasted_iota(jnp.int32, flat, 1)
    base = lane_flat - lane_flat % NBP
    diag = row == col
    trace = jnp.sum(jnp.where(diag, re, 0.0), axis=1, keepdims=True)
    level = group_sum(jnp.broadcast_to(trace, shape).reshape(flat), lane_flat).reshape(shape) / NB
    level = jnp.where(real, level, 1.0)
    re = re + jnp.where(diag, level, 0.0)
    for j in range(NB):
        index = base + j
        col_re = jnp.take_along_axis(re.reshape(flat), index, axis=1).reshape(shape)
        col_im = jnp.take_along_axis(im.reshape(flat), index, axis=1).reshape(shape)
        inverse = 1.0 / col_re[:, j : j + 1]
        here = (col == j)[:, j : j + 1]
        row_re = jnp.where(here, inverse, re[:, j : j + 1] * inverse)
        row_im = jnp.where(here, 0.0, im[:, j : j + 1] * inverse)
        cross = (row == j) | (col == j)
        col_re = jnp.where(row == j, -1.0, col_re)
        col_im = jnp.where(row == j, 0.0, col_im)
        re = jnp.where(cross, 0.0, re) - (col_re * row_re - col_im * row_im)
        im = jnp.where(cross, 0.0, im) - (col_re * row_im + col_im * row_re)
    return jnp.where(diag, 1.0, 0.0) - level * re, level * im


def filters_kernel(
    n, snap_ref, tab_hbm, w_hbm, wtd_hbm, f_hbm,
    tab_ref, w_ref, wtd_ref, f_ref, own_sem, wtd_sem, f_own,
    x_ref, s_ref, g_ref, got_ref, tot_ref,
    x_own, x_send, x_recv, g_send, g_recv, f_send, f_recv,
):
    me = lax.axis_index("space")
    rows = snap_ref.shape[0]
    cells = w_ref.shape[1]
    pieces = cells // CHUNK
    slots = -(-GROUPS // n)

    def peer(i):
        return lax.rem(me + i, n)

    def piece(there, h):
        return snap_ref.at[:, pl.ds(pl.multiple_of(there * cells + h * CHUNK, CHUNK), CHUNK)]

    x_mine = pl.ds(pl.multiple_of(me * rows, rows), rows)

    def local(h):
        return pltpu.make_async_copy(piece(me, h), x_ref.at[h, x_mine], x_own.at[h])

    def write(h):
        cols = pl.ds(pl.multiple_of(h * CHUNK, CHUNK), CHUNK)
        return pltpu.make_async_copy(wtd_ref.at[h], wtd_hbm.at[:, :, :, cols], wtd_sem.at[h])

    def exchange(i, h):
        there = peer((n + 1) // 2 + jnp.where(i % 2 == 1, (i - 1) // 2, -(i // 2)))
        return pltpu.make_async_remote_copy(
            src_ref=piece(there, h),
            dst_ref=x_ref.at[h, x_mine],
            send_sem=x_send.at[h, i],
            recv_sem=x_recv.at[h, i],
            device_id={"space": there},
            device_id_type=MESH,
        )

    def scatter(g):
        return pltpu.make_async_remote_copy(
            src_ref=g_ref.at[g],
            dst_ref=got_ref.at[g // n, me],
            send_sem=g_send.at[g],
            recv_sem=g_recv.at[g // n, me],
            device_id={"space": lax.rem(g, n)},
            device_id_type=MESH,
        )

    def scattered(slot, source):
        return pltpu.make_async_remote_copy(
            src_ref=g_ref.at[0],
            dst_ref=got_ref.at[slot, source],
            send_sem=g_send.at[0],
            recv_sem=g_recv.at[slot, source],
            device_id={"space": source},
            device_id_type=MESH,
        )

    def keep(slot):
        return pltpu.make_async_copy(f_ref.at[slot], f_hbm.at[slot * n + me], f_own.at[slot])

    def gather(g, i):
        return pltpu.make_async_remote_copy(
            src_ref=f_ref.at[g // n],
            dst_ref=f_hbm.at[g],
            send_sem=f_send.at[g // n, i],
            recv_sem=f_recv.at[g],
            device_id={"space": peer(i)},
            device_id_type=MESH,
        )

    barrier = pltpu.get_barrier_semaphore()

    @pl.loop(1, n)
    def _(i):
        pl.semaphore_signal(barrier, inc=1, device_id={"space": peer(i)}, device_id_type=MESH)

    for h in range(pieces):
        local(h).start()
    pl.semaphore_wait(barrier, n - 1)

    @pl.loop(0, pieces)
    def _(h):
        @pl.loop(1, n)
        def _(i):
            exchange(i, h).start()

    constants = (
        pltpu.make_async_copy(tab_hbm, tab_ref, own_sem.at[0]),
        pltpu.make_async_copy(w_hbm, w_ref, own_sem.at[1]),
    )
    for copy in constants:
        copy.start()
    g_ref[...] = jnp.zeros_like(g_ref)
    for p in range(2):
        for i in range(CHUNK // LANES):
            s_ref[p, i, pl.ds(NB, FP, stride=NBP), :] = jnp.zeros((FP, LANES), jnp.float32)

    for copy in constants:
        copy.wait()

    @pl.loop(0, pieces)
    def _(h):
        @pl.loop(1, n)
        def _(i):
            exchange(i, h).wait_recv()

        local(h).wait()
        dft_chunk(tab_ref, x_ref, w_ref, s_ref, h)

        @pl.loop(0, GROUPS, unroll=GROUPS)
        def _(g):
            gram_group(s_ref, wtd_ref, g_ref, h, g)

        write(h).start()

    @pl.loop(0, GROUPS)
    def _(g):
        @pl.when(lax.rem(g, n) != me)
        def _():
            scatter(g).start()

    for slot in range(slots):
        g = slot * n + me

        @pl.when(g < GROUPS)
        def _():
            tot_ref[slot] = g_ref[g]

            @pl.loop(1, n)
            def _(i):
                source = peer(i)
                scattered(slot, source).wait_recv()
                tot_ref[slot] += got_ref[slot, source]

        @pl.when(g >= GROUPS)
        def _():
            tot_ref[slot] = jnp.zeros((NBP, LANES), jnp.float32)

    shape = (slots, NBP, LANES)
    freq = (lax.broadcasted_iota(jnp.int32, shape, 0) * n + me) * GROUP + lax.broadcasted_iota(
        jnp.int32, shape, 2
    ) // NBP
    row = lax.broadcasted_iota(jnp.int32, (1, NBP, LANES), 1)
    col = lax.broadcasted_iota(jnp.int32, (1, NBP, LANES), 2) % NBP
    swapped = jnp.stack([fold(spread(tot_ref[slot]).T) for slot in range(slots)])
    same, other = invert(*unpack(tot_ref[...], swapped, row, col), freq < FREQS)
    filters = jnp.where(row <= col, same, other).astype(jnp.bfloat16)
    for slot in range(slots):
        g = slot * n + me

        @pl.when(g < GROUPS)
        def _():
            f_ref[slot] = filters[slot]
            keep(slot).start()

            @pl.loop(1, n)
            def _(i):
                gather(g, i).start()

    @pl.loop(0, pieces)
    def _(h):
        @pl.loop(1, n)
        def _(i):
            exchange(i, h).wait_send()

        write(h).wait()

    @pl.loop(0, GROUPS)
    def _(g):
        @pl.when(lax.rem(g, n) != me)
        def _():
            scatter(g).wait_send()
            gather(g, 0).wait_recv()

    for slot in range(slots):
        g = slot * n + me

        @pl.when(g < GROUPS)
        def _():
            @pl.loop(1, n)
            def _(i):
                gather(g, i).wait_send()

            keep(slot).wait()


def modes_kernel(f_ref, w_ref, wtd_ref, out_ref, mix_ref):
    cells = w_ref.shape[1]
    tiles = cells // LANES
    inverse_root = 1.0 / jnp.sqrt(w_ref[...])
    row = lax.broadcasted_iota(jnp.int32, (LANES, LANES), 0) % NBP
    col = lax.broadcasted_iota(jnp.int32, (LANES, LANES), 1) % NBP
    rows = 2 * tiles * NBP
    for s in range(GS):
        packed = spread(f_ref[s].astype(jnp.float32))
        same, other = unpack(packed, packed.T, row, col)
        filters = jnp.concatenate(
            (jnp.concatenate((same, other), axis=1), jnp.concatenate((-other, same), axis=1)), axis=0
        ).astype(jnp.bfloat16)
        wtd = wtd_ref[:, s * GROUP : (s + 1) * GROUP].reshape(2 * LANES, cells)
        mixed = jnp.dot(filters, wtd, preferred_element_type=jnp.float32) * inverse_root
        for q in range(2):
            for i in range(tiles):
                mix_ref[s, pl.ds(2 * i + q, LANES, stride=2 * tiles), :] = mixed[
                    q * LANES : (q + 1) * LANES, i * LANES : (i + 1) * LANES
                ]
        for k in range(GROUP):
            out_ref[s * GROUP + k] = mix_ref[s, k * rows : k * rows + 2 * tiles * NB, :].astype(jnp.bfloat16)


def per_device(snapshots, weights):
    n = lax.axis_size("space")
    rows = snapshots.shape[0]
    cells = snapshots.shape[1] // n
    pieces = cells // CHUNK
    tiles = cells // LANES
    slots = -(-GROUPS // n)
    table = jnp.asarray(make_table())
    w = weights.reshape(1, cells)
    dma = pltpu.SemaphoreType.DMA
    wtd, filters = pl.pallas_call(
        functools.partial(filters_kernel, n),
        out_shape=(
            jax.ShapeDtypeStruct((2, FP, NBP, cells), jnp.bfloat16),
            jax.ShapeDtypeStruct((GROUPS, NBP, LANES), jnp.bfloat16),
        ),
        in_specs=[pl.BlockSpec(memory_space=pltpu.HBM)] * 3,
        out_specs=(pl.BlockSpec(memory_space=pl.ANY),) * 2,
        scratch_shapes=[
            pltpu.VMEM(table.shape, table.dtype),
            pltpu.VMEM(w.shape, w.dtype),
            pltpu.VMEM((pieces, 2, FP, NBP, CHUNK), jnp.bfloat16),
            pltpu.VMEM((slots, NBP, LANES), jnp.bfloat16),
            dma((2,)),
            dma((pieces,)),
            dma((slots,)),
            pltpu.VMEM((pieces, n * rows, CHUNK), jnp.bfloat16),
            pltpu.VMEM((2, CHUNK // LANES, (FP + 1) * NBP, LANES), jnp.float32),
            pltpu.VMEM((GROUPS, NBP, LANES), jnp.float32),
            pltpu.VMEM((slots, n, NBP, LANES), jnp.float32),
            pltpu.VMEM((slots, NBP, LANES), jnp.float32),
            dma((pieces,)),
            dma((pieces, n)),
            dma((pieces, n)),
            dma((GROUPS,)),
            dma((slots, n)),
            dma((slots, n)),
            dma((GROUPS,)),
        ],
        compiler_params=pltpu.CompilerParams(
            collective_id=0, has_side_effects=True, vmem_limit_bytes=VLIM << 20
        ),
        name="filters",
    )(snapshots, table, w)
    modes = pl.pallas_call(
        modes_kernel,
        grid=(-(-GROUPS // GS),),
        out_shape=jax.ShapeDtypeStruct((FREQS, 2 * tiles * NB, LANES), jnp.bfloat16),
        in_specs=[
            pl.BlockSpec((GS, NBP, LANES), lambda g: (g, 0, 0)),
            VMEM,
            pl.BlockSpec((2, GS * GROUP, NBP, cells), lambda g: (0, g, 0, 0)),
        ],
        out_specs=pl.BlockSpec((GS * GROUP, 2 * tiles * NB, LANES), lambda g: (g, 0, 0)),
        scratch_shapes=[pltpu.VMEM((GS, 2 * tiles * (LANES + 1), LANES), jnp.float32)],
        compiler_params=pltpu.CompilerParams(vmem_limit_bytes=VLIM << 20),
        name="modes",
    )(filters, w, wtd)
    modes = modes.reshape(FREQS, NB, tiles, 2, LANES)
    return modes.transpose(3, 0, 1, 2, 4).reshape(2, FREQS, NB, cells)


def solution(mesh):
    return jax.shard_map(
        per_device,
        mesh=mesh,
        in_specs=(P("space", "slab"), P(("slab", "space"))),
        out_specs=P(None, None, None, ("slab", "space")),
        check_vma=False,
    )
```
